256 devices in a mesh: gz: 64 (over y, z, core), gy: 4 (over x).
Axes of the slice: x: 4, y: 4, z: 8, core: 2. Of those that a mesh axis runs over, the one named last changes fastest.
Arguments:
- field: bfloat16 [64, 32, 512, 512], P('gz', None, None, 'gy'), may hold values from -6 to 6
- spectral_weight: bfloat16 [2, 32, 1024, 1024], P(None, 'gy', 'gz'), may hold values from -16 to 16
- skip_weight: bfloat16 [32, 32], replicated, may hold values from -1 to 1
- skip_bias: float32 [32], replicated, may hold values from -3 to 3
Outputs:
- output: bfloat16 [64, 32, 512, 512], P('gz', None, None, 'gy')
The draws below stay inside these ranges and needn't reach their ends.
All inputs are finite; a program needn't handle non-finite values.
Results may differ from the reference program's by a relative error of at most 0.0041.
Values sent between devices are 32-bit elements; how exact they have to be, the bound alone decides.
No kernel may reach another device: no remote copies, remote signals or barrier semaphores. Data moves between devices by JAX's collectives and lax.ppermute only.
A program may use at most 192 MiB of HBM per device.

```python
import math
import jax
import jax.numpy as jnp
from jax import lax

NX = 512
NY = 512
C = 32
MX = 32
MY = 32
MZ = 32
NZ = 64


def shard_levels(stream_key, extent, split, smallest, largest):
    loudness, own = 1.0, jax.random.fold_in(stream_key, 6)
    for axis_at, parts in split:
        steps = jnp.exp(jax.random.uniform(jax.random.fold_in(own, axis_at), (parts,), jnp.float32, smallest / len(split), largest / len(split)))
        loudness = loudness * jnp.repeat(steps, extent[axis_at] // parts).reshape([-1 if axis == axis_at else 1 for axis in range(len(extent))])
    return loudness


def scatter_about(key, shape, deviation, most, cuts=(), held_as=jnp.bfloat16):
    level = shard_levels(key, shape, cuts, -0.22, 0.18) if cuts else 1.0
    drawn = jax.random.normal(key, shape, jnp.float32) * deviation * level
    return jnp.minimum(jnp.maximum(drawn, -most), most).astype(held_as)


def setup_inputs(seed: int = 0) -> dict:
    splits = jax.random.split(jax.random.key(seed), 5)
    return {
        "field": scatter_about(splits[0], (NZ, C, NX, NY), 1.0, 6.0, ((0, 64), (3, 4))),
        "spectral_weight": scatter_about(splits[1], (2, MX, MY * MZ, C * C), (0.7 * (NX * NY * NZ // (C * MX * MY * MZ)) ** 0.5), 16.0, ((1, 4), (2, 64))),
        "skip_weight": scatter_about(splits[2], (C, C), C ** -0.5, 1.0),
        "skip_bias": scatter_about(splits[3], (C,), 0.5, 3.0, (), jnp.float32),
    }


def frequencies(count):
    index = jnp.arange(count, dtype=jnp.int32)
    return jnp.where(index < count // 2, index, index - count).astype(jnp.int32)


def phases(freqs, positions, length):
    product = jnp.mod(positions[:, None] * freqs[None, :], length)
    angle = product.astype(jnp.float32) * (2.0 * math.pi / length)
    return jnp.cos(angle), jnp.sin(angle)


def x_table(count, modes):
    cos_x, sin_x = phases(frequencies(modes), jnp.arange(count, dtype=jnp.int32), count)
    return jnp.concatenate([cos_x.T, -sin_x.T], axis=0).astype(jnp.bfloat16)


def reference(field, spectral_weight, skip_weight, skip_bias):
    high = lax.Precision.HIGHEST
    xtable = x_table(NX, MX)
    xtable_wide = xtable.astype(jnp.float32)
    skip_wide = skip_weight.astype(jnp.float32)
    cos_y, sin_y = phases(frequencies(MY), jnp.arange(NY, dtype=jnp.int32), NY)
    cos_z, sin_z = phases(frequencies(MZ), jnp.arange(NZ, dtype=jnp.int32), NZ)

    def forward_plane(plane):
        along_x = jnp.einsum('qx,cxy->qcy', xtable_wide, plane.astype(jnp.float32), precision=high)
        along_x = along_x.reshape(2, MX, C, NY)
        with_cos = jnp.einsum('pacy,yk->pkac', along_x, cos_y, precision=high)
        with_sin = jnp.einsum('pacy,yk->pkac', along_x, sin_y, precision=high)
        return (with_cos[0] + with_sin[1], with_cos[1] - with_sin[0])

    part_r, part_i = lax.map(forward_plane, field)
    spec_r = jnp.einsum('zk,zyac->ykac', cos_z, part_r, precision=high) + jnp.einsum('zk,zyac->ykac', sin_z, part_i, precision=high)
    spec_i = jnp.einsum('zk,zyac->ykac', cos_z, part_i, precision=high) - jnp.einsum('zk,zyac->ykac', sin_z, part_r, precision=high)
    weights = spectral_weight.astype(jnp.float32).reshape(2, MX, MY, MZ, C, C)
    mix_r = jnp.einsum('ykac,aykco->ykao', spec_r, weights[0], precision=high) - jnp.einsum('ykac,aykco->ykao', spec_i, weights[1], precision=high)
    mix_i = jnp.einsum('ykac,aykco->ykao', spec_r, weights[1], precision=high) + jnp.einsum('ykac,aykco->ykao', spec_i, weights[0], precision=high)
    scale = 1.0 / (NX * NY * NZ)

    def inverse_plane(inputs):
        plane, cos_row, sin_row = inputs
        back_r = jnp.einsum('ykac,k->yac', mix_r, cos_row, precision=high) - jnp.einsum('ykac,k->yac', mix_i, sin_row, precision=high)
        back_i = jnp.einsum('ykac,k->yac', mix_i, cos_row, precision=high) + jnp.einsum('ykac,k->yac', mix_r, sin_row, precision=high)
        half_r = jnp.einsum('yac,ny->acn', back_r, cos_y, precision=high) - jnp.einsum('yac,ny->acn', back_i, sin_y, precision=high)
        half_i = jnp.einsum('yac,ny->acn', back_i, cos_y, precision=high) + jnp.einsum('yac,ny->acn', back_r, sin_y, precision=high)
        stacked = (jnp.stack([half_r, half_i], axis=0) * scale).astype(jnp.bfloat16).reshape(2 * MX, C, NY)
        spectral = jnp.einsum('qx,qcn->cxn', xtable_wide, stacked.astype(jnp.float32), precision=high)
        skipped = jnp.einsum('co,cxn->oxn', skip_wide, plane.astype(jnp.float32), precision=high)
        total = spectral + skipped + skip_bias[:, None, None]
        return jax.nn.gelu(total, approximate=False).astype(jnp.bfloat16)

    return lax.map(inverse_plane, (field, cos_z, sin_z))
```

```python
import functools
import math

import jax
import jax.numpy as jnp
import ml_dtypes
import numpy as np
from jax import lax
from jax.experimental import pallas as pl
from jax.experimental.pallas import tpu as pltpu
from jax.sharding import PartitionSpec as P

NX = 512
NY = 512
NZ = 64
C = 32
MODES = 32
PARTS_Y = 4
PARTS_Z = 64
ROWS_Y = NY // PARTS_Y
KX = MODES // PARTS_Y
KZ = MODES * MODES // PARTS_Z
HALF = C // 2
LANES = HALF * KX
X_BLOCK = 64
C_BLOCK = 8
H_ROWS = 80
F32 = jnp.float32
BF16 = jnp.bfloat16
TABLE = ml_dtypes.bfloat16


def phase_table(length):
    index = np.arange(MODES)
    freqs = np.where(index < MODES // 2, index, index - MODES)
    product = np.mod(freqs[:, None] * np.arange(length)[None, :], length)
    angle = product.astype(np.float32) * np.float32(2.0 * math.pi / length)
    return np.cos(angle).astype(np.float32), np.sin(angle).astype(np.float32)


def split_table(table):
    hi = table.astype(TABLE)
    lo = (table - hi.astype(np.float32)).astype(TABLE)
    return hi, lo


def forward_tables():
    cos_x, sin_x = phase_table(NX)
    rows = [part[b * KX : (b + 1) * KX] for b in range(PARTS_Y) for part in (cos_x, -sin_x)]
    xtable = np.concatenate(rows, axis=0).astype(TABLE)
    cos_y, sin_y = phase_table(NY)
    hi, lo = split_table(np.concatenate([cos_y, sin_y], axis=0))
    both = np.concatenate([hi, lo], axis=0).reshape(4 * MODES, PARTS_Y, ROWS_Y)
    return xtable, np.ascontiguousarray(both.transpose(1, 0, 2))


def middle_tables():
    cos_z, sin_z = phase_table(NZ)
    into, back = [], []
    for h in range(2):
        cos_h, sin_h = cos_z[h * KZ : (h + 1) * KZ], sin_z[h * KZ : (h + 1) * KZ]
        hi, lo = split_table(np.concatenate([cos_h, sin_h], axis=0))
        into.append(np.concatenate([hi, hi, lo], axis=1))
        hi, lo = split_table(np.concatenate([cos_h, -sin_h], axis=0).T)
        back.append(np.concatenate([hi, hi, lo], axis=1))
    channel = np.arange(LANES) // KX
    spread = (channel[:, None] == np.arange(HALF * C)[None, :] // C).astype(TABLE)
    column = np.arange(2 * LANES) // KX
    gather = (np.arange(4 * C)[:, None] % C == column[None, :]).astype(TABLE)
    return (
        np.stack(into),
        np.stack(back),
        np.concatenate([spread, spread], axis=0),
        np.concatenate([gather, gather], axis=0),
    )


def inverse_tables():
    cos_x, sin_x = phase_table(NX)
    rows = [part[b * KX : (b + 1) * KX] for b in range(PARTS_Y) for part in (cos_x, -sin_x)]
    ones = np.zeros((H_ROWS - 2 * MODES, NX), np.float32)
    ones[:3] = 1.0
    xback = np.concatenate(rows + [ones], axis=0).astype(TABLE).T
    cos_y, sin_y = phase_table(NY)
    scale = np.float32(1.0 / (NX * NY * NZ))
    tables = []
    for b in range(PARTS_Y):
        own = slice(b * ROWS_Y, (b + 1) * ROWS_Y)
        hi, lo = split_table(np.concatenate([cos_y[:, own], sin_y[:, own]], axis=1) * scale)
        tables.append(np.concatenate([hi, hi, lo], axis=0))
    return np.ascontiguousarray(xback), np.stack(tables)


def split(value):
    hi = value.astype(BF16)
    lo = (value - hi.astype(F32)).astype(BF16)
    return hi, lo


def dot(left, right, contract=((1,), (0,))):
    return lax.dot_general(left, right, (contract, ((), ())), preferred_element_type=F32)


def forward_kernel(field_ref, xtable_ref, ytable_ref, *refs):
    out_refs, along_ref = refs[:PARTS_Y], refs[PARTS_Y]
    step = pl.program_id(0)
    xtable = xtable_ref[...]
    for pair in range(C_BLOCK // 2):
        planes = jnp.concatenate([field_ref[0, 2 * pair], field_ref[0, 2 * pair + 1]], axis=1)
        along = dot(xtable, planes)
        for side in range(2):
            row = pl.multiple_of((step * C_BLOCK + 2 * pair + side) * KX, KX)
            for group in range(2 * PARTS_Y):
                along_ref[group, pl.ds(row, KX), :] = along[
                    group * KX : (group + 1) * KX, side * ROWS_Y : (side + 1) * ROWS_Y
                ]

    @pl.when(step == pl.num_programs(0) - 1)
    def _():
        me = lax.axis_index("gy")
        own = ytable_ref[me]
        table = jnp.concatenate([own, own], axis=1)
        for k in range(PARTS_Y):
            b = lax.rem(me + k, PARTS_Y)
            sums = []
            for part in range(2):
                hi, lo = split(along_ref[2 * b + part])
                both = jnp.concatenate([hi, lo], axis=1)
                full = dot(table, both, ((1,), (1,)))
                sums.append(full[: 2 * MODES] + full[2 * MODES :])
            real = sums[0][:MODES] + sums[1][MODES:]
            imag = sums[1][:MODES] - sums[0][MODES:]
            for at, value in ((0, real), (2, imag)):
                for half in range(2):
                    out_refs[k][pl.ds(at + half, MODES, stride=4), :] = value[
                        :, half * LANES : (half + 1) * LANES
                    ]


def middle_kernel(recv_ref, weight_ref, into_ref, back_ref, spread_ref, gather_ref, out_ref):
    h = lax.rem(lax.axis_index("gz"), 2)
    planes = jnp.concatenate(
        [recv_ref[pl.ds(j, PARTS_Z, stride=4), :] for j in range(4)], axis=1
    )
    hi, lo = split(planes)
    sums = dot(into_ref[h], jnp.concatenate([hi, lo, hi], axis=0))
    width = 2 * LANES
    real = sums[:KZ, :width] + sums[KZ:, width:]
    imag = sums[:KZ, width:] - sums[KZ:, :width]
    lane = lax.rem(lax.broadcasted_iota(jnp.int32, (KZ, width), 1), KX)
    picks = [lane == kx for kx in range(KX)]
    rows = jnp.concatenate(
        [jnp.where(pick, part, 0.0) for part in (real, imag) for pick in picks], axis=0
    )
    hi, lo = split(rows)
    modes = KX * KZ
    acc_r = jnp.zeros((modes, 4 * C), F32)
    acc_i = jnp.zeros((modes, 4 * C), F32)
    for half in range(2):
        cut = slice(half * LANES, (half + 1) * LANES)
        wide = dot(jnp.concatenate([hi[:, cut], lo[:, cut]], axis=1), spread_ref[...])
        for block in range(4):
            lanes = slice(block * 4 * C, (block + 1) * 4 * C)
            first = half * HALF * C + block * 4 * C
            w_r = weight_ref[0, :, :, first : first + 4 * C].reshape(modes, 4 * C).astype(F32)
            w_i = weight_ref[1, :, :, first : first + 4 * C].reshape(modes, 4 * C).astype(F32)
            f_r, f_i = wide[:modes, lanes], wide[modes:, lanes]
            acc_r = acc_r + (f_r * w_r - f_i * w_i)
            acc_i = acc_i + (f_r * w_i + f_i * w_r)
    hi, lo = split(jnp.concatenate([acc_r, acc_i], axis=0))
    mixed = dot(jnp.concatenate([hi, lo], axis=1), gather_ref[...])
    parts = []
    for part in range(2):
        total = jnp.zeros((KZ, width), F32)
        for kx in range(KX):
            first = part * modes + kx * KZ
            total = total + jnp.where(picks[kx], mixed[first : first + KZ], 0.0)
        parts.append(total)
    turned = jnp.concatenate(
        [jnp.concatenate(parts, axis=1), jnp.concatenate([parts[1], -parts[0]], axis=1)], axis=0
    )
    hi, lo = split(turned)
    result = dot(back_ref[h], jnp.concatenate([hi, lo, hi], axis=0))
    for j in range(4):
        out_ref[pl.ds(j, PARTS_Z, stride=4), :] = result[:, j * LANES : (j + 1) * LANES]


def gelu(value):
    return value * (0.5 + 0.5 * lax.erf(value * math.sqrt(0.5)))


def inverse_kernel(
    r0, r1, r2, r3, field_ref, ytable_ref, xback_ref, skip_ref, bias_ref, out_ref,
    spectrum_ref, kron_ref, skipped_ref,
):
    @pl.when(pl.program_id(0) == 0)
    def _():
        me = lax.axis_index("gy")
        table = ytable_ref[me]
        for k, block in enumerate((r0, r1, r2, r3)):
            b = lax.rem(me + PARTS_Y - k, PARTS_Y)
            at = pl.multiple_of(b * 2 * KX, 2 * KX)
            for half in range(2):
                sums = []
                for part in range(2):
                    hi, lo = split(block[pl.ds(2 * part + half, MODES, stride=4), :])
                    rows = jnp.concatenate([hi, lo, hi], axis=0)
                    sums.append(dot(rows, table, ((0,), (0,))))
                real = sums[0][:, :ROWS_Y] - sums[1][:, ROWS_Y:]
                imag = sums[1][:, :ROWS_Y] + sums[0][:, ROWS_Y:]
                for o in range(HALF):
                    rows = slice(o * KX, (o + 1) * KX)
                    spectrum_ref[half * HALF + o, pl.ds(at, 2 * KX), :] = jnp.concatenate(
                        [real[rows], imag[rows]], axis=0
                    ).astype(BF16)
        row = lax.broadcasted_iota(jnp.int32, (H_ROWS - 2 * MODES, ROWS_Y), 0)
        for o in range(C):
            bias = jnp.full((H_ROWS - 2 * MODES, ROWS_Y), bias_ref[o], F32)
            hi = bias.astype(BF16).astype(F32)
            mid = (bias - hi).astype(BF16).astype(F32)
            low = bias - hi - mid
            pieces = jnp.where(row == 0, hi, jnp.where(row == 1, mid, jnp.where(row == 2, low, 0.0)))
            spectrum_ref[o, 2 * MODES : H_ROWS, :] = pieces.astype(BF16)
        size = 16 * C
        out_row = lax.broadcasted_iota(jnp.int32, (size, C), 0)
        out_col = lax.broadcasted_iota(jnp.int32, (size, C), 1)
        rows_of = (out_row // 16 == out_col).astype(F32).astype(BF16)
        wide = dot(rows_of, skip_ref[...], ((1,), (1,))).astype(BF16)
        wide = dot(wide, rows_of, ((1,), (1,)))
        i = lax.broadcasted_iota(jnp.int32, (size, size), 0)
        j = lax.broadcasted_iota(jnp.int32, (size, size), 1)
        same = lax.rem(i, 16) == lax.rem(j, 16)
        kron_ref[...] = jnp.where(same, wide, 0.0).astype(BF16)

    first = pl.multiple_of(pl.program_id(0) * X_BLOCK, X_BLOCK)
    groups = X_BLOCK // 16
    for pair in range(groups // 2):
        planes = jnp.concatenate(
            [
                field_ref[0, :, (2 * pair + side) * 16 : (2 * pair + side + 1) * 16, :].reshape(
                    16 * C, ROWS_Y
                )
                for side in range(2)
            ],
            axis=1,
        )
        skipped_ref[:, pair * 2 * ROWS_Y : (pair + 1) * 2 * ROWS_Y] = dot(kron_ref[...], planes)
    table = xback_ref[pl.ds(first, X_BLOCK), :]

    @pl.loop(0, C // 2)
    def _(pair):
        o = pair * 2
        both = jnp.concatenate([spectrum_ref[o], spectrum_ref[o + 1]], axis=1)
        spectral = dot(table, both)
        for side in range(2):
            row = pl.multiple_of((o + side) * 16, 16)
            for g in range(groups):
                total = (
                    spectral[g * 16 : (g + 1) * 16, side * ROWS_Y : (side + 1) * ROWS_Y]
                    + skipped_ref[pl.ds(row, 16), g * ROWS_Y : (g + 1) * ROWS_Y]
                )
                out_ref[0, o + side, g * 16 : (g + 1) * 16, :] = gelu(total).astype(BF16)


def whole(shape):
    return pl.BlockSpec(shape, lambda *_: (0,) * len(shape))


def per_device(field, spectral_weight, skip_weight, skip_bias):
    block = jax.ShapeDtypeStruct((4 * MODES, LANES), F32)
    xtable, ytable = forward_tables()
    parts = pl.pallas_call(
        forward_kernel,
        grid=(C // C_BLOCK,),
        in_specs=[
            pl.BlockSpec((1, C_BLOCK, NX, ROWS_Y), lambda i: (0, i, 0, 0)),
            whole(xtable.shape),
            whole(ytable.shape),
        ],
        out_specs=[whole(block.shape)] * PARTS_Y,
        out_shape=[block] * PARTS_Y,
        scratch_shapes=[pltpu.VMEM((2 * PARTS_Y, C * KX, ROWS_Y), F32)],
        compiler_params=pltpu.CompilerParams(vmem_limit_bytes=32 * 1024 * 1024),
        name="forward",
    )(field, jnp.asarray(xtable), jnp.asarray(ytable))
    turns = [[(i, (i + k) % PARTS_Y) for i in range(PARTS_Y)] for k in range(PARTS_Y)]
    total = parts[0]
    for k in range(1, PARTS_Y):
        total = total + lax.ppermute(parts[k], "gy", turns[k])
    sent = jnp.broadcast_to(total.reshape(MODES, 1, 4, LANES), (MODES, 2, 4, LANES))
    got = lax.all_to_all(sent.reshape(PARTS_Z, 4, LANES), "gz", 0, 0, tiled=True)
    into, back, spread, gather = middle_tables()
    mixed = pl.pallas_call(
        middle_kernel,
        out_shape=jax.ShapeDtypeStruct((PARTS_Z * 4, LANES), F32),
        compiler_params=pltpu.CompilerParams(vmem_limit_bytes=32 * 1024 * 1024),
        name="middle",
    )(
        got.reshape(PARTS_Z * 4, LANES),
        spectral_weight,
        jnp.asarray(into),
        jnp.asarray(back),
        jnp.asarray(spread),
        jnp.asarray(gather),
    )
    got = lax.all_to_all(mixed.reshape(PARTS_Z, 4, LANES), "gz", 0, 0, tiled=True)
    got = got.reshape(MODES, 2, 4, LANES)
    mine = (got[:, 0] + got[:, 1]).reshape(4 * MODES, LANES)
    blocks = [mine] + [lax.ppermute(mine, "gy", turns[k]) for k in range(1, PARTS_Y)]
    xback, yback = inverse_tables()
    tile = pl.BlockSpec((1, C, X_BLOCK, ROWS_Y), lambda i: (0, 0, i, 0))
    return pl.pallas_call(
        inverse_kernel,
        grid=(NX // X_BLOCK,),
        in_specs=[whole(block.shape)] * PARTS_Y
        + [
            tile,
            whole(yback.shape),
            whole(xback.shape),
            whole(skip_weight.shape),
            pl.BlockSpec(memory_space=pltpu.SMEM),
        ],
        out_specs=tile,
        out_shape=jax.ShapeDtypeStruct(field.shape, BF16),
        scratch_shapes=[
            pltpu.VMEM((C, H_ROWS, ROWS_Y), BF16),
            pltpu.VMEM((16 * C, 16 * C), BF16),
            pltpu.VMEM((16 * C, X_BLOCK // 16 * ROWS_Y), F32),
        ],
        compiler_params=pltpu.CompilerParams(vmem_limit_bytes=32 * 1024 * 1024),
        name="inverse",
    )(*blocks, field, jnp.asarray(yback), jnp.asarray(xback), skip_weight, skip_bias)


def solution(mesh):
    placed = (P("gz", None, None, "gy"), P(None, "gy", "gz", None), P(), P())
    return jax.shard_map(
        per_device, mesh=mesh, in_specs=placed, out_specs=P("gz", None, None, "gy"), check_vma=False
    )
```

```python
import functools
import math

import jax
import jax.numpy as jnp
import ml_dtypes
import numpy as np
from jax import lax
from jax.experimental import pallas as pl
from jax.experimental.pallas import tpu as pltpu
from jax.sharding import PartitionSpec as P

NX = 512
NY = 512
NZ = 64
C = 32
MODES = 32
PARTS_Y = 4
PARTS_Z = 64
ROWS_Y = NY // PARTS_Y
KX = MODES // PARTS_Y
KZ = MODES * MODES // PARTS_Z
HALF = C // 2
LANES = HALF * KX
X_BLOCK = 128
O_BLOCK = 16
S_BLOCK = 128
CHUNKS = (8, 8, 8, 8)
H_ROWS = 80
F32 = jnp.float32
BF16 = jnp.bfloat16
TABLE = ml_dtypes.bfloat16


def phase_table(length):
    index = np.arange(MODES)
    freqs = np.where(index < MODES // 2, index, index - MODES)
    product = np.mod(freqs[:, None] * np.arange(length)[None, :], length)
    angle = product.astype(np.float32) * np.float32(2.0 * math.pi / length)
    return np.cos(angle).astype(np.float32), np.sin(angle).astype(np.float32)


def split_table(table):
    hi = table.astype(TABLE)
    lo = (table - hi.astype(np.float32)).astype(TABLE)
    return hi, lo


def forward_tables():
    cos_x, sin_x = phase_table(NX)
    rows = [part[b * KX : (b + 1) * KX] for b in range(PARTS_Y) for part in (cos_x, -sin_x)]
    xtable = np.concatenate(rows, axis=0).astype(TABLE)
    cos_y, sin_y = phase_table(NY)
    hi, lo = split_table(np.concatenate([cos_y, sin_y], axis=0))
    both = np.concatenate([hi, lo], axis=0).reshape(4 * MODES, PARTS_Y, ROWS_Y)
    return xtable, np.ascontiguousarray(both.transpose(1, 0, 2))


def middle_tables():
    cos_z, sin_z = phase_table(NZ)
    into, back = [], []
    for h in range(2):
        cos_h, sin_h = cos_z[h * KZ : (h + 1) * KZ], sin_z[h * KZ : (h + 1) * KZ]
        hi, lo = split_table(np.concatenate([cos_h, sin_h], axis=0))
        into.append(np.concatenate([hi, hi, lo], axis=1))
        hi, lo = split_table(np.concatenate([cos_h, -sin_h], axis=0).T)
        back.append(np.concatenate([hi, hi, lo], axis=1))
    channel = np.arange(LANES) // KX
    spread = (channel[:, None] == np.arange(HALF * C)[None, :] // C).astype(TABLE)
    column = np.arange(2 * LANES) // KX
    gather = (np.arange(4 * C)[:, None] % C == column[None, :]).astype(TABLE)
    table = np.zeros((6 * MODES * 2, 6 * LANES), TABLE)
    table[: 2 * LANES, : 4 * LANES] = np.concatenate([spread, spread], axis=0)
    table[: 2 * LANES, 4 * LANES :] = np.concatenate([gather, gather], axis=0)
    for h in range(2):
        first = 2 * LANES + h * PARTS_Z
        table[first : first + 2 * KZ, : 3 * PARTS_Z] = into[h]
        table[first : first + PARTS_Z, 2 * LANES : 2 * LANES + 6 * KZ] = back[h]
    return table


def inverse_tables():
    cos_x, sin_x = phase_table(NX)
    rows = [part[b * KX : (b + 1) * KX] for b in range(PARTS_Y) for part in (cos_x, -sin_x)]
    ones = np.zeros((H_ROWS - 2 * MODES, NX), np.float32)
    ones[:3] = 1.0
    xback = (0.5 * np.concatenate(rows + [ones], axis=0).astype(TABLE).astype(np.float32)).T
    xback = np.pad(xback, ((0, 0), (0, 2 * ROWS_Y - H_ROWS))).astype(TABLE)
    cos_y, sin_y = phase_table(NY)
    scale = np.float32(1.0 / (NX * NY * NZ))
    tables = [xback]
    for b in range(PARTS_Y):
        own = slice(b * ROWS_Y, (b + 1) * ROWS_Y)
        hi, lo = split_table(np.concatenate([cos_y[:, own], sin_y[:, own]], axis=1) * scale)
        tables.append(np.concatenate([hi, hi, lo], axis=0))
    return np.concatenate(tables, axis=0)


def split(value):
    hi = value.astype(BF16)
    lo = (value - hi.astype(F32)).astype(BF16)
    return hi, lo


def dot(left, right, contract=((1,), (0,))):
    return lax.dot_general(left, right, (contract, ((), ())), preferred_element_type=F32)


def forward_kernel(field_ref, xtable_ref, ytable_ref, *refs):
    out_refs = refs[:PARTS_Y]
    xrows_ref, yrows_ref, planes_ref, along_ref, sems = refs[PARTS_Y:]
    me = lax.axis_index("gy")
    chunk_count = len(CHUNKS)
    edges = np.cumsum((0,) + CHUNKS).tolist()
    tables = [
        pltpu.make_async_copy(xtable_ref, xrows_ref, sems.at[chunk_count]),
        pltpu.make_async_copy(ytable_ref.at[me], yrows_ref, sems.at[chunk_count + 1]),
    ]
    chunks = [
        pltpu.make_async_copy(
            field_ref.at[0, pl.ds(edges[i], CHUNKS[i])],
            planes_ref.at[pl.ds(edges[i], CHUNKS[i])],
            sems.at[i],
        )
        for i in range(chunk_count)
    ]
    for copy in tables + chunks:
        copy.start()
    for copy in tables:
        copy.wait()
    xtable = xrows_ref[...]
    own = yrows_ref[...]
    table = jnp.concatenate([own, own], axis=1)
    for i in range(chunk_count):
        chunks[i].wait()
        for first in range(edges[i], edges[i + 1], 2):
            planes = jnp.concatenate([planes_ref[first], planes_ref[first + 1]], axis=1)
            along = dot(xtable, planes)
            for side in range(2):
                rows = slice((first + side) * KX, (first + side + 1) * KX)
                for group in range(2 * PARTS_Y):
                    along_ref[group, rows, :] = along[
                        group * KX : (group + 1) * KX, side * ROWS_Y : (side + 1) * ROWS_Y
                    ]
        for half, k in [
            (half, k)
            for half in range(2)
            if edges[i] < (half + 1) * HALF <= edges[i + 1]
            for k in range(PARTS_Y)
        ]:
            b = lax.rem(me + k, PARTS_Y)
            sums = []
            for part in range(2):
                hi, lo = split(along_ref[2 * b + part, half * LANES : (half + 1) * LANES, :])
                both = jnp.concatenate([hi, lo], axis=1)
                full = dot(table, both, ((1,), (1,)))
                sums.append(full[: 2 * MODES] + full[2 * MODES :])
            out_refs[k][pl.ds(half, MODES, stride=4), :] = sums[0][:MODES] + sums[1][MODES:]
            out_refs[k][pl.ds(2 + half, MODES, stride=4), :] = sums[1][:MODES] - sums[0][MODES:]


def middle_kernel(recv_ref, weight_ref, table_ref, out_ref):
    h = lax.rem(lax.axis_index("gz"), 2)
    own = pl.multiple_of(2 * LANES + h * PARTS_Z, PARTS_Z)
    into = table_ref[pl.ds(own, 2 * KZ), : 3 * PARTS_Z]
    back = table_ref[pl.ds(own, PARTS_Z), 2 * LANES : 2 * LANES + 6 * KZ]
    spread = table_ref[: 2 * LANES, : 4 * LANES]
    gather = table_ref[: 2 * LANES, 4 * LANES :]
    planes = jnp.concatenate(
        [recv_ref[pl.ds(j, PARTS_Z, stride=4), :] for j in range(4)], axis=1
    )
    hi, lo = split(planes)
    sums = dot(into, jnp.concatenate([hi, lo, hi], axis=0))
    width = 2 * LANES
    real = sums[:KZ, :width] + sums[KZ:, width:]
    imag = sums[:KZ, width:] - sums[KZ:, :width]
    lane = lax.rem(lax.broadcasted_iota(jnp.int32, (KZ, width), 1), KX)
    picks = [lane == kx for kx in range(KX)]
    rows = jnp.concatenate(
        [jnp.where(pick, part, 0.0) for part in (real, imag) for pick in picks], axis=0
    )
    hi, lo = split(rows)
    modes = KX * KZ
    acc_r = jnp.zeros((modes, 4 * C), F32)
    acc_i = jnp.zeros((modes, 4 * C), F32)
    for half in range(2):
        cut = slice(half * LANES, (half + 1) * LANES)
        wide = dot(jnp.concatenate([hi[:, cut], lo[:, cut]], axis=1), spread)
        for block in range(4):
            lanes = slice(block * 4 * C, (block + 1) * 4 * C)
            first = half * HALF * C + block * 4 * C
            w_r = weight_ref[0, :, :, first : first + 4 * C].reshape(modes, 4 * C).astype(F32)
            w_i = weight_ref[1, :, :, first : first + 4 * C].reshape(modes, 4 * C).astype(F32)
            f_r, f_i = wide[:modes, lanes], wide[modes:, lanes]
            acc_r = acc_r + (f_r * w_r - f_i * w_i)
            acc_i = acc_i + (f_r * w_i + f_i * w_r)
    hi, lo = split(jnp.concatenate([acc_r, acc_i], axis=0))
    mixed = dot(jnp.concatenate([hi, lo], axis=1), gather)
    parts = []
    for part in range(2):
        total = jnp.zeros((KZ, width), F32)
        for kx in range(KX):
            first = part * modes + kx * KZ
            total = total + jnp.where(picks[kx], mixed[first : first + KZ], 0.0)
        parts.append(total)
    turned = jnp.concatenate(
        [jnp.concatenate(parts, axis=1), jnp.concatenate([parts[1], -parts[0]], axis=1)], axis=0
    )
    hi, lo = split(turned)
    result = dot(back, jnp.concatenate([hi, lo, hi], axis=0))
    for j in range(4):
        out_ref[pl.ds(j, PARTS_Z, stride=4), :] = result[:, j * LANES : (j + 1) * LANES]


def gelu(half):
    return half * lax.erf(half * math.sqrt(2.0)) + half


def prepare_kernel(skip_ref, bias_ref, kron_ref, bias_rows_ref):
    row = lax.broadcasted_iota(jnp.int32, (16, ROWS_Y), 0)
    for o in range(C):
        bias = jnp.full((16, ROWS_Y), bias_ref[o], F32)
        hi = bias.astype(BF16).astype(F32)
        mid = (bias - hi).astype(BF16).astype(F32)
        low = bias - hi - mid
        pieces = jnp.where(row == 0, hi, jnp.where(row == 1, mid, jnp.where(row == 2, low, 0.0)))
        bias_rows_ref[o] = pieces.astype(BF16)
    size = 8 * C
    out_row = lax.broadcasted_iota(jnp.int32, (size, C), 0)
    out_col = lax.broadcasted_iota(jnp.int32, (size, C), 1)
    rows_of = (out_row // 8 == out_col).astype(F32).astype(BF16)
    wide = dot(rows_of, skip_ref[...], ((1,), (1,))).astype(BF16)
    wide = dot(wide, rows_of, ((1,), (1,)))
    i = lax.broadcasted_iota(jnp.int32, (size, size), 0)
    j = lax.broadcasted_iota(jnp.int32, (size, size), 1)
    same = lax.rem(i, 8) == lax.rem(j, 8)
    kron_ref[...] = jnp.where(same, wide * 0.5, 0.0).astype(BF16)


def skip_kernel(after_ref, field_ref, kron_ref, out_ref, planes_ref, sems):
    del after_ref
    copies = [
        pltpu.make_async_copy(
            field_ref.at[0, :, pl.ds(step * S_BLOCK, S_BLOCK)],
            planes_ref.at[:, pl.ds(step * S_BLOCK, S_BLOCK)],
            sems.at[step],
        )
        for step in range(NX // S_BLOCK)
    ]
    for copy in copies:
        copy.start()
    for step, copy in enumerate(copies):
        copy.wait()
        for first in range(step * S_BLOCK, (step + 1) * S_BLOCK, 32):
            groups = []
            for at in (first, first + 16):
                wide = planes_ref[:, at : at + 16, :].astype(F32)
                groups += [wide[:, :8].reshape(8 * C, ROWS_Y), wide[:, 8:].reshape(8 * C, ROWS_Y)]
            skipped = dot(kron_ref[...], jnp.concatenate(groups, axis=1).astype(BF16))
            for g in range(4):
                out_ref[:, first + 8 * g : first + 8 * (g + 1), :] = skipped[
                    :, g * ROWS_Y : (g + 1) * ROWS_Y
                ].reshape(C, 8, ROWS_Y)


def collect_kernel(p0, p1, p2, p3, after_ref, out_ref):
    del after_ref
    for j in range(4):
        rows = pl.ds(j, MODES, stride=4)
        total = p0[rows, :] + p1[rows, :] + p2[rows, :] + p3[rows, :]
        for h in range(2):
            out_ref[pl.ds(4 * h + j, MODES, stride=8), :] = total


def pairs_kernel(recv_ref, out_ref):
    for j in range(4):
        first, second = [recv_ref[pl.ds(4 * h + j, MODES, stride=8), :] for h in range(2)]
        out_ref[pl.ds(j, MODES, stride=4), :] = first + second


def inverse_kernel(
    r0, r1, r2, r3, skipped_ref, table_ref, bias_ref, out_ref, spectrum_ref, tile_ref, sems
):
    me = lax.axis_index("gy")
    start = pl.multiple_of(NX + me * 3 * MODES, 32)
    table = table_ref[pl.ds(start, 3 * MODES), :]
    for k, block in enumerate((r0, r1, r2, r3)):
        b = lax.rem(me + PARTS_Y - k, PARTS_Y)
        at = pl.multiple_of(b * 2 * KX, 2 * KX)
        for half in range(2):
            sums = []
            for part in range(2):
                hi, lo = split(block[pl.ds(2 * part + half, MODES, stride=4), :])
                rows = jnp.concatenate([hi, lo, hi], axis=0)
                sums.append(dot(rows, table, ((0,), (0,))))
            real = sums[0][:, :ROWS_Y] - sums[1][:, ROWS_Y:]
            imag = sums[1][:, :ROWS_Y] + sums[0][:, ROWS_Y:]
            for o in range(HALF):
                rows = slice(o * KX, (o + 1) * KX)
                spectrum_ref[half * HALF + o, pl.ds(at, 2 * KX), :] = jnp.concatenate(
                    [real[rows], imag[rows]], axis=0
                ).astype(BF16)

    def copy_out(o):
        rows = pl.ds(o, 2)
        return pltpu.make_async_copy(tile_ref.at[rows], out_ref.at[0, rows], sems.at[o // 2])

    @pl.loop(0, C, step=O_BLOCK)
    def _(block_first):
        for pair in range(O_BLOCK // 2):
            o = block_first + 2 * pair
            both = jnp.concatenate(
                [
                    jnp.concatenate([spectrum_ref[o + side], bias_ref[o + side]], axis=0)
                    for side in range(2)
                ],
                axis=1,
            )
            for first in range(0, NX, X_BLOCK):
                rows = slice(first, first + X_BLOCK)
                spectral = dot(table_ref[rows, :H_ROWS], both)
                for side in range(2):
                    total = (
                        spectral[:, side * ROWS_Y : (side + 1) * ROWS_Y]
                        + skipped_ref[o + side, rows, :]
                    )
                    tile_ref[o + side, rows, :] = gelu(total).astype(BF16)
            copy_out(o).start()

    for o in range(0, C, 2):
        copy_out(o).wait()


def in_place(value):
    return pltpu.with_memory_space_constraint(value, pltpu.HBM)


def whole(shape):
    return pl.BlockSpec(shape, lambda *_: (0,) * len(shape))


def forward(field):
    block = jax.ShapeDtypeStruct((4 * MODES, LANES), F32)
    xtable, ytable = forward_tables()
    in_hbm = pl.BlockSpec(memory_space=pltpu.HBM)
    return pl.pallas_call(
        forward_kernel,
        in_specs=[in_hbm] * 3,
        out_shape=[block] * PARTS_Y,
        scratch_shapes=[
            pltpu.VMEM(xtable.shape, BF16),
            pltpu.VMEM(ytable.shape[1:], BF16),
            pltpu.VMEM((C, NX, ROWS_Y), BF16),
            pltpu.VMEM((2 * PARTS_Y, C * KX, ROWS_Y), F32),
            pltpu.SemaphoreType.DMA((len(CHUNKS) + 2,)),
        ],
        compiler_params=pltpu.CompilerParams(vmem_limit_bytes=16 * 1024 * 1024),
        name="forward",
    )(in_place(field), in_place(jnp.asarray(xtable)), in_place(jnp.asarray(ytable)))


def per_device(field, spectral_weight, skip_weight, skip_bias):
    block = jax.ShapeDtypeStruct((4 * MODES, LANES), F32)
    parts = forward(field)
    turns = [[(i, (i + k) % PARTS_Y) for i in range(PARTS_Y)] for k in range(PARTS_Y)]
    kron, bias_rows = prepare(skip_weight, skip_bias)
    parts = [parts[0]] + [lax.ppermute(parts[k], "gy", turns[k]) for k in range(1, PARTS_Y)]
    small = pltpu.CompilerParams(vmem_limit_bytes=12 * 1024 * 1024)
    spread = jax.ShapeDtypeStruct((PARTS_Z * 4, LANES), F32)
    sent = pl.pallas_call(
        collect_kernel,
        in_specs=[pl.BlockSpec(memory_space=pltpu.VMEM)] * PARTS_Y
        + [pl.BlockSpec(memory_space=pl.ANY)],
        out_shape=spread,
        compiler_params=small,
        name="collect",
    )(*parts, kron)
    got = lax.all_to_all(sent.reshape(PARTS_Z, 4, LANES), "gz", 0, 0, tiled=True)
    mixed = pl.pallas_call(
        middle_kernel,
        out_shape=spread,
        compiler_params=small,
        name="middle",
    )(got.reshape(PARTS_Z * 4, LANES), spectral_weight, jnp.asarray(middle_tables()))
    got = lax.all_to_all(mixed.reshape(PARTS_Z, 4, LANES), "gz", 0, 0, tiled=True)
    mine = pl.pallas_call(
        pairs_kernel,
        out_shape=block,
        compiler_params=small,
        name="pairs",
    )(got.reshape(PARTS_Z * 4, LANES))
    blocks = [mine] + [lax.ppermute(mine, "gy", turns[k]) for k in range(1, PARTS_Y)]
    return inverse(blocks, skip(mine, field, kron), bias_rows)


def prepare(skip_weight, skip_bias):
    return pl.pallas_call(
        prepare_kernel,
        in_specs=[
            pl.BlockSpec(memory_space=pltpu.VMEM),
            pl.BlockSpec(memory_space=pltpu.SMEM),
        ],
        out_shape=[
            jax.ShapeDtypeStruct((8 * C, 8 * C), BF16),
            jax.ShapeDtypeStruct((C, 16, ROWS_Y), BF16),
        ],
        compiler_params=pltpu.CompilerParams(vmem_limit_bytes=12 * 1024 * 1024),
        cost_estimate=pl.CostEstimate(flops=10**9, bytes_accessed=10**6, transcendentals=0),
        name="prepare",
    )(skip_weight, skip_bias)


def skip(after, field, kron):
    return pl.pallas_call(
        skip_kernel,
        in_specs=[
            pl.BlockSpec(memory_space=pl.ANY),
            pl.BlockSpec(memory_space=pltpu.HBM),
            pl.BlockSpec(memory_space=pltpu.VMEM),
        ],
        out_shape=jax.ShapeDtypeStruct((C, NX, ROWS_Y), F32),
        scratch_shapes=[
            pltpu.VMEM((C, NX, ROWS_Y), BF16),
            pltpu.SemaphoreType.DMA((NX // S_BLOCK,)),
        ],
        compiler_params=pltpu.CompilerParams(vmem_limit_bytes=16 * 1024 * 1024),
        cost_estimate=pl.CostEstimate(flops=2 * 10**9, bytes_accessed=10**7, transcendentals=0),
        name="skip",
    )(after, in_place(field), kron)


def inverse(blocks, skipped, bias_rows):
    table = inverse_tables()
    return pl.pallas_call(
        inverse_kernel,
        out_specs=pl.BlockSpec(memory_space=pltpu.HBM),
        out_shape=jax.ShapeDtypeStruct((1, C, NX, ROWS_Y), BF16),
        scratch_shapes=[
            pltpu.VMEM((C, 2 * MODES, ROWS_Y), BF16),
            pltpu.VMEM((C, NX, ROWS_Y), BF16),
            pltpu.SemaphoreType.DMA((C // 2,)),
        ],
        compiler_params=pltpu.CompilerParams(vmem_limit_bytes=12 * 1024 * 1024),
        name="inverse",
    )(*blocks, skipped, jnp.asarray(table), bias_rows)


def solution(mesh):
    placed = (P("gz", None, None, "gy"), P(None, "gy", "gz", None), P(), P())
    return jax.shard_map(
        per_device, mesh=mesh, in_specs=placed, out_specs=P("gz", None, None, "gy"), check_vma=False
    )
```

```python
import functools
import math

import jax
import jax.numpy as jnp
import ml_dtypes
import numpy as np
from jax import lax
from jax.experimental import pallas as pl
from jax.experimental.pallas import tpu as pltpu
from jax.sharding import PartitionSpec as P

NX = 512
NY = 512
NZ = 64
C = 32
MODES = 32
PARTS_Y = 4
PARTS_Z = 64
ROWS_Y = NY // PARTS_Y
KX = MODES // PARTS_Y
HALF_KX = KX // 2
KZ = MODES * MODES // PARTS_Z
HALF = C // 2
LANES = HALF * KX
X_BLOCK = 128
O_BLOCK = 16
S_BLOCK = 128
CHUNKS = (8, 8, 8, 8)
H_ROWS = 80
F32 = jnp.float32
BF16 = jnp.bfloat16
TABLE = ml_dtypes.bfloat16


def phase_table(length):
    index = np.arange(MODES)
    freqs = np.where(index < MODES // 2, index, index - MODES)
    product = np.mod(freqs[:, None] * np.arange(length)[None, :], length)
    angle = product.astype(np.float32) * np.float32(2.0 * math.pi / length)
    return np.cos(angle).astype(np.float32), np.sin(angle).astype(np.float32)


def split_table(table):
    hi = table.astype(TABLE)
    lo = (table - hi.astype(np.float32)).astype(TABLE)
    return hi, lo


def forward_tables():
    cos_x, sin_x = phase_table(NX)
    rows = [part[g * HALF_KX : (g + 1) * HALF_KX] for g in range(2 * PARTS_Y) for part in (cos_x, -sin_x)]
    xtable = np.concatenate(rows, axis=0).astype(TABLE)
    cos_y, sin_y = phase_table(NY)
    hi, lo = split_table(np.concatenate([cos_y, sin_y], axis=0))
    both = np.concatenate([hi, lo], axis=0).reshape(4 * MODES, PARTS_Y, ROWS_Y)
    return xtable, np.ascontiguousarray(both.transpose(1, 0, 2))


def middle_tables():
    cos_z, sin_z = phase_table(NZ)
    into, back = [], []
    for h in range(2):
        order = (np.arange(MODES) + h * KZ) % MODES
        cos_h, sin_h = cos_z[order], sin_z[order]
        hi, lo = split_table(np.concatenate([cos_h, sin_h], axis=0))
        into.append(np.concatenate([hi, hi, lo], axis=1))
        hi, lo = split_table(np.concatenate([cos_h, sin_h], axis=0).T)
        back.append(np.concatenate([hi, hi, lo], axis=1))
    channel = np.arange(LANES) // KX
    spread = (channel[:, None] == np.arange(HALF * C)[None, :] // C).astype(TABLE)
    column = np.arange(2 * LANES) // KX
    gather = (np.arange(4 * C)[:, None] % C == column[None, :]).astype(TABLE)
    table = np.zeros((6 * MODES * 2, 6 * LANES), TABLE)
    table[: 2 * LANES, : 4 * LANES] = np.concatenate([spread, spread], axis=0)
    table[: 2 * LANES, 4 * LANES :] = np.concatenate([gather, gather], axis=0)
    for h in range(2):
        first = 2 * LANES + h * PARTS_Z
        table[first : first + PARTS_Z, : 3 * PARTS_Z] = into[h]
        table[first : first + PARTS_Z, 2 * LANES : 2 * LANES + 6 * MODES] = back[h]
    return table


def inverse_tables():
    cos_x, sin_x = phase_table(NX)
    rows = [part[g * HALF_KX : (g + 1) * HALF_KX] for g in range(2 * PARTS_Y) for part in (cos_x, -sin_x)]
    ones = np.zeros((H_ROWS - 2 * MODES, NX), np.float32)
    ones[:3] = 1.0
    xback = (0.5 * np.concatenate(rows + [ones], axis=0).astype(TABLE).astype(np.float32)).T
    xback = np.pad(xback, ((0, 0), (0, ROWS_Y - H_ROWS))).astype(TABLE)
    cos_y, sin_y = phase_table(NY)
    scale = np.float32(1.0 / (NX * NY * NZ))
    tables = [xback]
    for b in range(PARTS_Y):
        own = slice(b * ROWS_Y, (b + 1) * ROWS_Y)
        for part in (cos_y, sin_y):
            hi, lo = split_table(part[:, own] * scale)
            tables.append(np.concatenate([hi, hi, lo], axis=0))
    return np.concatenate(tables, axis=0)


def split(value):
    hi = value.astype(BF16)
    lo = (value - hi.astype(F32)).astype(BF16)
    return hi, lo


def turn(value, sign):
    first = lax.rem(lax.broadcasted_iota(jnp.int32, (value.shape[0], LANES), 1), KX) < HALF_KX
    parts = []
    for at in range(0, value.shape[1], LANES):
        part = value[:, at : at + LANES]
        ahead = pltpu.roll(part, LANES - HALF_KX, axis=1)
        behind = pltpu.roll(part, HALF_KX, axis=1)
        parts.append(jnp.where(first, sign * ahead, -sign * behind))
    return jnp.concatenate(parts, axis=1) if len(parts) > 1 else parts[0]


def dot(left, right, contract=((1,), (0,))):
    return lax.dot_general(left, right, (contract, ((), ())), preferred_element_type=F32)


def forward_kernel(field_ref, xtable_ref, ytable_ref, weight_ref, *refs):
    out_refs = refs[:PARTS_Y]
    send_ref, xrows_ref, yrows_ref, weights_ref, planes_ref, along_ref, sems = refs[PARTS_Y:]
    h = lax.rem(lax.axis_index("gz"), 2)
    me = lax.axis_index("gy")
    chunk_count = len(CHUNKS)
    edges = np.cumsum((0,) + CHUNKS).tolist()
    tables = [
        pltpu.make_async_copy(xtable_ref, xrows_ref, sems.at[chunk_count]),
        pltpu.make_async_copy(ytable_ref.at[me], yrows_ref, sems.at[chunk_count + 1]),
    ]
    chunks = [
        pltpu.make_async_copy(
            field_ref.at[0, pl.ds(edges[i], CHUNKS[i])],
            planes_ref.at[pl.ds(edges[i], CHUNKS[i])],
            sems.at[i],
        )
        for i in range(chunk_count)
    ]
    weights = pltpu.make_async_copy(
        weight_ref.at[:, pl.ds((1 - h) * HALF_KX, HALF_KX)], weights_ref, sems.at[chunk_count + 2]
    )
    for copy in tables + chunks[:2] + [weights] + chunks[2:]:
        copy.start()
    for copy in tables:
        copy.wait()
    xtable = xrows_ref[...]
    own = yrows_ref[...]
    table = jnp.concatenate([own, own], axis=1)
    for i in range(chunk_count):
        chunks[i].wait()
        for first in range(edges[i], edges[i + 1], 2):
            planes = jnp.concatenate([planes_ref[first], planes_ref[first + 1]], axis=1)
            along = dot(xtable, planes)
            for side in range(2):
                rows = slice((first + side) * KX, (first + side + 1) * KX)
                for group in range(2 * PARTS_Y):
                    along_ref[group, rows, :] = along[
                        group * KX : (group + 1) * KX, side * ROWS_Y : (side + 1) * ROWS_Y
                    ]
        if i == 2:
            weights.wait()
            send_ref[...] = weights_ref[...].astype(F32)
        for half, k in [
            (half, k)
            for half in range(2)
            if edges[i] < (half + 1) * HALF <= edges[i + 1]
            for k in range(PARTS_Y)
        ]:
            b = lax.rem(me + k, PARTS_Y)
            for side in range(2):
                hi, lo = split(along_ref[2 * b + side, half * LANES : (half + 1) * LANES, :])
                both = jnp.concatenate([hi, lo], axis=1)
                full = dot(table, both, ((1,), (1,)))
                sums = full[: 2 * MODES] + full[2 * MODES :]
                out_refs[k][pl.ds(2 * side + half, MODES, stride=4), :] = sums[:MODES] + turn(
                    sums[MODES:], 1.0
                )


def middle_kernel(recv_ref, weight_ref, other_ref, table_ref, out_ref):
    h = lax.rem(lax.axis_index("gz"), 2)
    own = pl.multiple_of(2 * LANES + h * PARTS_Z, PARTS_Z)
    into = table_ref[pl.ds(own, PARTS_Z), : 3 * PARTS_Z]
    back = table_ref[pl.ds(own, PARTS_Z), 2 * LANES : 2 * LANES + 6 * MODES]
    spread = table_ref[: 2 * LANES, : 4 * LANES]
    gather = table_ref[: 2 * LANES, 4 * LANES :]
    planes = jnp.concatenate(
        [recv_ref[pl.ds(half, PARTS_Z, stride=2), :] for half in range(2)], axis=1
    )
    hi, lo = split(planes)
    sums = dot(into, jnp.concatenate([hi, lo, hi], axis=0))
    spectrum = sums[:MODES] + turn(sums[MODES:], 1.0)
    lane = lax.rem(lax.broadcasted_iota(jnp.int32, spectrum.shape, 1), KX)
    picks = [lane == at for at in range(KX)]
    rows = jnp.concatenate([jnp.where(pick, spectrum, 0.0) for pick in picks], axis=0)
    hi, lo = split(rows)
    modes = HALF_KX * MODES
    acc_r = jnp.zeros((modes, 4 * C), F32)
    acc_i = jnp.zeros((modes, 4 * C), F32)
    for half in range(2):
        cut = slice(half * LANES, (half + 1) * LANES)
        wide = dot(jnp.concatenate([hi[:, cut], lo[:, cut]], axis=1), spread)
        for block in range(4):
            lanes = slice(block * 4 * C, (block + 1) * 4 * C)
            first = half * HALF * C + block * 4 * C
            w_r, w_i = [
                jnp.concatenate(
                    [
                        weight_ref[part, pl.ds(h * HALF_KX, HALF_KX), :, first : first + 4 * C].astype(F32),
                        other_ref[part, :, :, first : first + 4 * C],
                    ],
                    axis=1,
                ).reshape(modes, 4 * C)
                for part in range(2)
            ]
            f_r, f_i = wide[:modes, lanes], wide[modes:, lanes]
            acc_r = acc_r + (f_r * w_r - f_i * w_i)
            acc_i = acc_i + (f_r * w_i + f_i * w_r)
    hi, lo = split(jnp.concatenate([acc_r, acc_i], axis=0))
    mixed = dot(jnp.concatenate([hi, lo], axis=1), gather)
    total = jnp.zeros(spectrum.shape, F32)
    for at, pick in enumerate(picks):
        total = total + jnp.where(pick, mixed[at * MODES : (at + 1) * MODES], 0.0)
    hi, lo = split(jnp.concatenate([total, turn(total, -1.0)], axis=0))
    result = dot(back, jnp.concatenate([hi, lo, hi], axis=0))
    for half in range(2):
        out_ref[pl.ds(half, PARTS_Z, stride=2), :] = result[:, half * LANES : (half + 1) * LANES]


def gelu(half):
    return half * lax.erf(half * math.sqrt(2.0)) + half


def prepare_kernel(skip_ref, bias_ref, kron_ref, bias_rows_ref):
    row = lax.broadcasted_iota(jnp.int32, (16, ROWS_Y), 0)
    for o in range(C):
        bias = jnp.full((16, ROWS_Y), bias_ref[o], F32)
        hi = bias.astype(BF16).astype(F32)
        mid = (bias - hi).astype(BF16).astype(F32)
        low = bias - hi - mid
        pieces = jnp.where(row == 0, hi, jnp.where(row == 1, mid, jnp.where(row == 2, low, 0.0)))
        bias_rows_ref[o] = pieces.astype(BF16)
    size = 8 * C
    out_row = lax.broadcasted_iota(jnp.int32, (size, C), 0)
    out_col = lax.broadcasted_iota(jnp.int32, (size, C), 1)
    rows_of = (out_row // 8 == out_col).astype(F32).astype(BF16)
    wide = dot(rows_of, skip_ref[...], ((1,), (1,))).astype(BF16)
    wide = dot(wide, rows_of, ((1,), (1,)))
    i = lax.broadcasted_iota(jnp.int32, (size, size), 0)
    j = lax.broadcasted_iota(jnp.int32, (size, size), 1)
    same = lax.rem(i, 8) == lax.rem(j, 8)
    kron_ref[...] = jnp.where(same, wide * 0.5, 0.0).astype(BF16)


def skip_kernel(after_ref, field_ref, kron_ref, out_ref, planes_ref, sems):
    del after_ref
    copies = [
        pltpu.make_async_copy(
            field_ref.at[0, :, pl.ds(step * S_BLOCK, S_BLOCK)],
            planes_ref.at[:, pl.ds(step * S_BLOCK, S_BLOCK)],
            sems.at[step],
        )
        for step in range(NX // S_BLOCK)
    ]
    for copy in copies:
        copy.start()
    for step, copy in enumerate(copies):
        copy.wait()
        for first in range(step * S_BLOCK, (step + 1) * S_BLOCK, 32):
            groups = []
            for at in (first, first + 16):
                wide = planes_ref[:, at : at + 16, :].astype(F32)
                groups += [wide[:, :8].reshape(8 * C, ROWS_Y), wide[:, 8:].reshape(8 * C, ROWS_Y)]
            skipped = dot(kron_ref[...], jnp.concatenate(groups, axis=1).astype(BF16))
            for g in range(4):
                out_ref[:, first + 8 * g : first + 8 * (g + 1), :] = skipped[
                    :, g * ROWS_Y : (g + 1) * ROWS_Y
                ].reshape(C, 8, ROWS_Y)


def collect_kernel(p0, p1, p2, p3, after_ref, out_ref):
    del after_ref
    out_ref[...] = p0[...] + p1[...] + p2[...] + p3[...]


def inverse_kernel(
    r0, r1, r2, r3, skipped_ref, table_ref, bias_ref, out_ref, spectrum_ref, tile_ref, sems
):
    me = lax.axis_index("gy")
    start = pl.multiple_of(NX + me * 6 * MODES, 6 * MODES)
    table = table_ref[pl.ds(start, 6 * MODES), :]
    for k, block in enumerate((r0, r1, r2, r3)):
        b = lax.rem(me + PARTS_Y - k, PARTS_Y)
        at = pl.multiple_of(b * 2 * KX, 2 * KX)
        for half in range(2):
            sides = []
            for side in range(2):
                value = block[pl.ds(2 * side + half, MODES, stride=4), :]
                pieces = [split(value), split(turn(value, -1.0))]
                rows = jnp.concatenate([v for hi, lo in pieces for v in (hi, lo, hi)], axis=0)
                sides.append(dot(rows, table, ((0,), (0,))))
            for o in range(HALF):
                rows = slice(o * KX, (o + 1) * KX)
                spectrum_ref[half * HALF + o, pl.ds(at, 2 * KX), :] = jnp.concatenate(
                    [sides[0][rows], sides[1][rows]], axis=0
                ).astype(BF16)

    def copy_out(o):
        rows = pl.ds(o, 2)
        return pltpu.make_async_copy(tile_ref.at[rows], out_ref.at[0, rows], sems.at[o // 2])

    @pl.loop(0, C, step=O_BLOCK)
    def _(block_first):
        for pair in range(O_BLOCK // 2):
            o = block_first + 2 * pair
            both = jnp.concatenate(
                [
                    jnp.concatenate([spectrum_ref[o + side], bias_ref[o + side]], axis=0)
                    for side in range(2)
                ],
                axis=1,
            )
            for first in range(0, NX, X_BLOCK):
                rows = slice(first, first + X_BLOCK)
                spectral = dot(table_ref[rows, :H_ROWS], both)
                for side in range(2):
                    total = (
                        spectral[:, side * ROWS_Y : (side + 1) * ROWS_Y]
                        + skipped_ref[o + side, rows, :]
                    )
                    tile_ref[o + side, rows, :] = gelu(total).astype(BF16)
            copy_out(o).start()

    for o in range(0, C, 2):
        copy_out(o).wait()


def in_place(value):
    return pltpu.with_memory_space_constraint(value, pltpu.HBM)


def whole(shape):
    return pl.BlockSpec(shape, lambda *_: (0,) * len(shape))


def forward(field, weight):
    block = jax.ShapeDtypeStruct((4 * MODES, LANES), F32)
    share = (2, HALF_KX, KZ, C * C)
    xtable, ytable = forward_tables()
    in_hbm = pl.BlockSpec(memory_space=pltpu.HBM)
    return pl.pallas_call(
        forward_kernel,
        in_specs=[in_hbm] * 4,
        out_shape=[block] * PARTS_Y + [jax.ShapeDtypeStruct(share, F32)],
        scratch_shapes=[
            pltpu.VMEM(xtable.shape, BF16),
            pltpu.VMEM(ytable.shape[1:], BF16),
            pltpu.VMEM(share, BF16),
            pltpu.VMEM((C, NX, ROWS_Y), BF16),
            pltpu.VMEM((2 * PARTS_Y, C * KX, ROWS_Y), F32),
            pltpu.SemaphoreType.DMA((len(CHUNKS) + 3,)),
        ],
        compiler_params=pltpu.CompilerParams(vmem_limit_bytes=16 * 1024 * 1024),
        name="forward",
    )(
        in_place(field),
        in_place(jnp.asarray(xtable)),
        in_place(jnp.asarray(ytable)),
        in_place(weight),
    )


def per_device(field, spectral_weight, skip_weight, skip_bias):
    block = jax.ShapeDtypeStruct((4 * MODES, LANES), F32)
    *parts, send = forward(field, spectral_weight)
    turns = [[(i, (i + k) % PARTS_Y) for i in range(PARTS_Y)] for k in range(PARTS_Y)]
    parts = [parts[0]] + [lax.ppermute(parts[k], "gy", turns[k]) for k in range(1, PARTS_Y)]
    kron, bias_rows = prepare(skip_weight, skip_bias)
    other = lax.ppermute(send, "gz", [(i, i ^ 1) for i in range(PARTS_Z)])
    small = pltpu.CompilerParams(vmem_limit_bytes=12 * 1024 * 1024)
    sent = pl.pallas_call(
        collect_kernel,
        in_specs=[pl.BlockSpec(memory_space=pltpu.VMEM)] * PARTS_Y
        + [pl.BlockSpec(memory_space=pl.ANY)],
        out_shape=block,
        compiler_params=small,
        name="collect",
    )(*parts, kron)
    got = lax.all_to_all(sent.reshape(PARTS_Z, 2, LANES), "gz", 0, 0, tiled=True)
    mixed = pl.pallas_call(
        middle_kernel,
        out_shape=block,
        compiler_params=small,
        name="middle",
    )(got.reshape(block.shape), spectral_weight, other, jnp.asarray(middle_tables()))
    got = lax.all_to_all(mixed.reshape(PARTS_Z, 2, LANES), "gz", 0, 0, tiled=True)
    mine = got.reshape(block.shape)
    blocks = [mine] + [lax.ppermute(mine, "gy", turns[k]) for k in range(1, PARTS_Y)]
    return inverse(blocks, skip(mine, field, kron), bias_rows)


def prepare(skip_weight, skip_bias):
    return pl.pallas_call(
        prepare_kernel,
        in_specs=[
            pl.BlockSpec(memory_space=pltpu.VMEM),
            pl.BlockSpec(memory_space=pltpu.SMEM),
        ],
        out_shape=[
            jax.ShapeDtypeStruct((8 * C, 8 * C), BF16),
            jax.ShapeDtypeStruct((C, 16, ROWS_Y), BF16),
        ],
        compiler_params=pltpu.CompilerParams(vmem_limit_bytes=12 * 1024 * 1024),
        cost_estimate=pl.CostEstimate(flops=10**9, bytes_accessed=10**6, transcendentals=0),
        name="prepare",
    )(skip_weight, skip_bias)


def skip(after, field, kron):
    return pl.pallas_call(
        skip_kernel,
        in_specs=[
            pl.BlockSpec(memory_space=pl.ANY),
            pl.BlockSpec(memory_space=pltpu.HBM),
            pl.BlockSpec(memory_space=pltpu.VMEM),
        ],
        out_shape=jax.ShapeDtypeStruct((C, NX, ROWS_Y), F32),
        scratch_shapes=[
            pltpu.VMEM((C, NX, ROWS_Y), BF16),
            pltpu.SemaphoreType.DMA((NX // S_BLOCK,)),
        ],
        compiler_params=pltpu.CompilerParams(vmem_limit_bytes=16 * 1024 * 1024),
        cost_estimate=pl.CostEstimate(flops=2 * 10**9, bytes_accessed=10**7, transcendentals=0),
        name="skip",
    )(after, in_place(field), kron)


def inverse(blocks, skipped, bias_rows):
    table = inverse_tables()
    return pl.pallas_call(
        inverse_kernel,
        out_specs=pl.BlockSpec(memory_space=pltpu.HBM),
        out_shape=jax.ShapeDtypeStruct((1, C, NX, ROWS_Y), BF16),
        scratch_shapes=[
            pltpu.VMEM((C, 2 * MODES, ROWS_Y), BF16),
            pltpu.VMEM((C, NX, ROWS_Y), BF16),
            pltpu.SemaphoreType.DMA((C // 2,)),
        ],
        compiler_params=pltpu.CompilerParams(vmem_limit_bytes=12 * 1024 * 1024),
        name="inverse",
    )(*blocks, skipped, jnp.asarray(table), bias_rows)


def solution(mesh):
    placed = (P("gz", None, None, "gy"), P(None, "gy", "gz", None), P(), P())
    return jax.shard_map(
        per_device, mesh=mesh, in_specs=placed, out_specs=P("gz", None, None, "gy"), check_vma=False
    )
```

```python
import functools
import math

import jax
import jax.numpy as jnp
import ml_dtypes
import numpy as np
from jax import lax
from jax.experimental import pallas as pl
from jax.experimental.pallas import tpu as pltpu
from jax.sharding import PartitionSpec as P

NX = 512
NY = 512
NZ = 64
C = 32
MODES = 32
PARTS_Y = 4
PARTS_Z = 64
ROWS_Y = NY // PARTS_Y
KX = MODES // PARTS_Y
HALF_KX = KX // 2
KZ = MODES * MODES // PARTS_Z
HALF = C // 2
LANES = HALF * KX
X_BLOCK = 128
O_BLOCK = 32
ORDER = (2, 1, 3)
BACK_ORDER = (3, 1, 2)
S_BLOCK = 128
CHUNKS = (8, 8, 8, 8)
H_ROWS = 80
F32 = jnp.float32
BF16 = jnp.bfloat16
TABLE = ml_dtypes.bfloat16


def phase_table(length):
    index = np.arange(MODES)
    freqs = np.where(index < MODES // 2, index, index - MODES)
    product = np.mod(freqs[:, None] * np.arange(length)[None, :], length)
    angle = product.astype(np.float32) * np.float32(2.0 * math.pi / length)
    return np.cos(angle).astype(np.float32), np.sin(angle).astype(np.float32)


def split_table(table):
    hi = table.astype(TABLE)
    lo = (table - hi.astype(np.float32)).astype(TABLE)
    return hi, lo


def forward_tables():
    cos_x, sin_x = phase_table(NX)
    rows = [part[g * HALF_KX : (g + 1) * HALF_KX] for g in range(2 * PARTS_Y) for part in (cos_x, -sin_x)]
    xtable = np.concatenate(rows, axis=0).astype(TABLE)
    cos_y, sin_y = phase_table(NY)
    hi, lo = split_table(np.concatenate([cos_y, sin_y], axis=0))
    both = np.concatenate([hi, lo], axis=0).reshape(4 * MODES, PARTS_Y, ROWS_Y)
    return xtable, np.ascontiguousarray(both.transpose(1, 0, 2))


def middle_tables():
    cos_z, sin_z = phase_table(NZ)
    into, back = [], []
    for h in range(2):
        order = (np.arange(MODES) + h * KZ) % MODES
        cos_h, sin_h = cos_z[order], sin_z[order]
        hi, lo = split_table(np.concatenate([cos_h, sin_h], axis=0))
        into.append(np.concatenate([hi, hi, lo], axis=1))
        hi, lo = split_table(np.concatenate([cos_h, sin_h], axis=0).T)
        back.append(np.concatenate([hi, hi, lo], axis=1))
    channel = np.arange(LANES) // KX
    spread = (channel[:, None] == np.arange(HALF * C)[None, :] // C).astype(TABLE)
    column = np.arange(2 * LANES) // KX
    gather = (np.arange(4 * C)[:, None] % C == column[None, :]).astype(TABLE)
    table = np.zeros((6 * MODES * 2, 6 * LANES), TABLE)
    table[: 2 * LANES, : 4 * LANES] = np.concatenate([spread, spread], axis=0)
    table[: 2 * LANES, 4 * LANES :] = np.concatenate([gather, gather], axis=0)
    for h in range(2):
        first = 2 * LANES + h * PARTS_Z
        table[first : first + PARTS_Z, : 3 * PARTS_Z] = into[h]
        table[first : first + PARTS_Z, 2 * LANES : 2 * LANES + 6 * MODES] = back[h]
    return table


def inverse_tables():
    cos_x, sin_x = phase_table(NX)
    rows = [part[g * HALF_KX : (g + 1) * HALF_KX] for g in range(2 * PARTS_Y) for part in (cos_x, -sin_x)]
    ones = np.zeros((H_ROWS - 2 * MODES, NX), np.float32)
    ones[:3] = 1.0
    xback = (0.5 * np.concatenate(rows + [ones], axis=0).astype(TABLE).astype(np.float32)).T
    xback = np.pad(xback, ((0, 0), (0, ROWS_Y - H_ROWS))).astype(TABLE)
    cos_y, sin_y = phase_table(NY)
    scale = np.float32(1.0 / (NX * NY * NZ))
    tables = [xback]
    for b in range(PARTS_Y):
        own = slice(b * ROWS_Y, (b + 1) * ROWS_Y)
        for part in (cos_y, sin_y):
            hi, lo = split_table(part[:, own] * scale)
            tables.append(np.concatenate([hi, hi, lo], axis=0))
    return np.concatenate(tables, axis=0)


def split(value):
    hi = value.astype(BF16)
    lo = (value - hi.astype(F32)).astype(BF16)
    return hi, lo


def turn(value, sign):
    first = lax.rem(lax.broadcasted_iota(jnp.int32, (value.shape[0], LANES), 1), KX) < HALF_KX
    parts = []
    for at in range(0, value.shape[1], LANES):
        part = value[:, at : at + LANES]
        ahead = pltpu.roll(part, LANES - HALF_KX, axis=1)
        behind = pltpu.roll(part, HALF_KX, axis=1)
        parts.append(jnp.where(first, sign * ahead, -sign * behind))
    return jnp.concatenate(parts, axis=1) if len(parts) > 1 else parts[0]


def dot(left, right, contract=((1,), (0,))):
    return lax.dot_general(left, right, (contract, ((), ())), preferred_element_type=F32)


def forward_kernel(field_ref, xtable_ref, ytable_ref, weight_ref, *refs):
    out_refs = refs[:PARTS_Y]
    send_ref, xrows_ref, yrows_ref, weights_ref, planes_ref, along_ref, sems = refs[PARTS_Y:]
    h = lax.rem(lax.axis_index("gz"), 2)
    me = lax.axis_index("gy")
    chunk_count = len(CHUNKS)
    edges = np.cumsum((0,) + CHUNKS).tolist()
    tables = [
        pltpu.make_async_copy(xtable_ref, xrows_ref, sems.at[chunk_count]),
        pltpu.make_async_copy(ytable_ref.at[me], yrows_ref, sems.at[chunk_count + 1]),
    ]
    chunks = [
        pltpu.make_async_copy(
            field_ref.at[0, pl.ds(edges[i], CHUNKS[i])],
            planes_ref.at[pl.ds(edges[i], CHUNKS[i])],
            sems.at[i],
        )
        for i in range(chunk_count)
    ]
    weights = pltpu.make_async_copy(
        weight_ref.at[:, pl.ds((1 - h) * HALF_KX, HALF_KX)], weights_ref, sems.at[chunk_count + 2]
    )
    for copy in tables + chunks[:2] + [weights] + chunks[2:]:
        copy.start()
    for copy in tables:
        copy.wait()
    xtable = xrows_ref[...]
    own = yrows_ref[...]
    table = jnp.concatenate([own, own], axis=1)
    for i in range(chunk_count):
        chunks[i].wait()
        for first in range(edges[i], edges[i + 1], 2):
            planes = jnp.concatenate([planes_ref[first], planes_ref[first + 1]], axis=1)
            along = dot(xtable, planes)
            for side in range(2):
                rows = slice((first + side) * KX, (first + side + 1) * KX)
                for group in range(2 * PARTS_Y):
                    along_ref[group, rows, :] = along[
                        group * KX : (group + 1) * KX, side * ROWS_Y : (side + 1) * ROWS_Y
                    ]
        if i == 2:
            weights.wait()
            send_ref[...] = weights_ref[...].astype(F32)
        for half, k in [
            (half, k)
            for half in range(2)
            if edges[i] < (half + 1) * HALF <= edges[i + 1]
            for k in range(PARTS_Y)
        ]:
            b = lax.rem(me + k, PARTS_Y)
            for side in range(2):
                hi, lo = split(along_ref[2 * b + side, half * LANES : (half + 1) * LANES, :])
                both = jnp.concatenate([hi, lo], axis=1)
                full = dot(table, both, ((1,), (1,)))
                sums = full[: 2 * MODES] + full[2 * MODES :]
                out_refs[k][pl.ds(2 * side + half, MODES, stride=4), :] = sums[:MODES] + turn(
                    sums[MODES:], 1.0
                )


def middle_kernel(recv_ref, weight_ref, other_ref, table_ref, out_ref):
    h = lax.rem(lax.axis_index("gz"), 2)
    own = pl.multiple_of(2 * LANES + h * PARTS_Z, PARTS_Z)
    into = table_ref[pl.ds(own, PARTS_Z), : 3 * PARTS_Z]
    back = table_ref[pl.ds(own, PARTS_Z), 2 * LANES : 2 * LANES + 6 * MODES]
    spread = table_ref[: 2 * LANES, : 4 * LANES]
    gather = table_ref[: 2 * LANES, 4 * LANES :]
    planes = jnp.concatenate(
        [recv_ref[pl.ds(half, PARTS_Z, stride=2), :] for half in range(2)], axis=1
    )
    hi, lo = split(planes)
    sums = dot(into, jnp.concatenate([hi, lo, hi], axis=0))
    spectrum = sums[:MODES] + turn(sums[MODES:], 1.0)
    lane = lax.rem(lax.broadcasted_iota(jnp.int32, spectrum.shape, 1), KX)
    picks = [lane == at for at in range(KX)]
    rows = jnp.concatenate([jnp.where(pick, spectrum, 0.0) for pick in picks], axis=0)
    hi, lo = split(rows)
    modes = HALF_KX * MODES
    acc_r = jnp.zeros((modes, 4 * C), F32)
    acc_i = jnp.zeros((modes, 4 * C), F32)
    for half in range(2):
        cut = slice(half * LANES, (half + 1) * LANES)
        wide = dot(jnp.concatenate([hi[:, cut], lo[:, cut]], axis=1), spread)
        for block in range(4):
            lanes = slice(block * 4 * C, (block + 1) * 4 * C)
            first = half * HALF * C + block * 4 * C
            w_r, w_i = [
                jnp.concatenate(
                    [
                        weight_ref[part, pl.ds(h * HALF_KX, HALF_KX), :, first : first + 4 * C].astype(F32),
                        other_ref[part, :, :, first : first + 4 * C],
                    ],
                    axis=1,
                ).reshape(modes, 4 * C)
                for part in range(2)
            ]
            f_r, f_i = wide[:modes, lanes], wide[modes:, lanes]
            acc_r = acc_r + (f_r * w_r - f_i * w_i)
            acc_i = acc_i + (f_r * w_i + f_i * w_r)
    hi, lo = split(jnp.concatenate([acc_r, acc_i], axis=0))
    mixed = dot(jnp.concatenate([hi, lo], axis=1), gather)
    total = jnp.zeros(spectrum.shape, F32)
    for at, pick in enumerate(picks):
        total = total + jnp.where(pick, mixed[at * MODES : (at + 1) * MODES], 0.0)
    hi, lo = split(jnp.concatenate([total, turn(total, -1.0)], axis=0))
    result = dot(back, jnp.concatenate([hi, lo, hi], axis=0))
    for half in range(2):
        out_ref[pl.ds(half, PARTS_Z, stride=2), :] = result[:, half * LANES : (half + 1) * LANES]


def gelu(half):
    return half * lax.erf(half * math.sqrt(2.0)) + half


def prepare_kernel(skip_ref, bias_ref, kron_ref, bias_rows_ref):
    row = lax.broadcasted_iota(jnp.int32, (16, ROWS_Y), 0)
    for o in range(C):
        bias = jnp.full((16, ROWS_Y), bias_ref[o], F32)
        hi = bias.astype(BF16).astype(F32)
        mid = (bias - hi).astype(BF16).astype(F32)
        low = bias - hi - mid
        pieces = jnp.where(row == 0, hi, jnp.where(row == 1, mid, jnp.where(row == 2, low, 0.0)))
        bias_rows_ref[o] = pieces.astype(BF16)
    size = 8 * C
    out_row = lax.broadcasted_iota(jnp.int32, (size, C), 0)
    out_col = lax.broadcasted_iota(jnp.int32, (size, C), 1)
    rows_of = (out_row // 8 == out_col).astype(F32).astype(BF16)
    wide = dot(rows_of, skip_ref[...], ((1,), (1,))).astype(BF16)
    wide = dot(wide, rows_of, ((1,), (1,)))
    i = lax.broadcasted_iota(jnp.int32, (size, size), 0)
    j = lax.broadcasted_iota(jnp.int32, (size, size), 1)
    same = lax.rem(i, 8) == lax.rem(j, 8)
    kron_ref[...] = jnp.where(same, wide * 0.5, 0.0).astype(BF16)


def skip_kernel(after_ref, field_ref, kron_ref, out_ref):
    del after_ref
    for first in range(0, NX, 32):
        groups = []
        for at in (first, first + 16):
            wide = field_ref[0, :, at : at + 16, :].astype(F32)
            groups += [wide[:, :8].reshape(8 * C, ROWS_Y), wide[:, 8:].reshape(8 * C, ROWS_Y)]
        skipped = dot(kron_ref[...], jnp.concatenate(groups, axis=1).astype(BF16))
        for g in range(4):
            out_ref[:, first + 8 * g : first + 8 * (g + 1), :] = skipped[
                :, g * ROWS_Y : (g + 1) * ROWS_Y
            ].reshape(C, 8, ROWS_Y)


def collect_kernel(p0, p1, p2, p3, after_ref, out_ref):
    del after_ref
    out_ref[...] = p0[...] + p1[...] + p2[...] + p3[...]


def inverse_kernel(
    r0, r1, r2, r3, skipped_ref, table_ref, bias_ref, out_ref, spectrum_ref, tile_ref, sems
):
    me = lax.axis_index("gy")
    start = pl.multiple_of(NX + me * 6 * MODES, 6 * MODES)
    table = table_ref[pl.ds(start, 6 * MODES), :]
    for k, block in zip((0,) + BACK_ORDER, (r0, r1, r2, r3)):
        b = lax.rem(me + PARTS_Y - k, PARTS_Y)
        at = pl.multiple_of(b * 2 * KX, 2 * KX)
        value = jnp.concatenate(
            [block[pl.ds(2 * side + half, MODES, stride=4), :] for half in range(2) for side in range(2)],
            axis=1,
        )
        pieces = [split(value), split(turn(value, -1.0))]
        rows = jnp.concatenate([v for hi, lo in pieces for v in (hi, lo, hi)], axis=0)
        full = dot(rows, table, ((0,), (0,)))
        for o in range(C):
            first = o // HALF * 2 * LANES + o % HALF * KX
            spectrum_ref[o, pl.ds(at, 2 * KX), :] = jnp.concatenate(
                [full[first : first + KX], full[first + LANES : first + LANES + KX]], axis=0
            ).astype(BF16)

    def copy_out(o):
        rows = pl.ds(o, 2)
        return pltpu.make_async_copy(tile_ref.at[rows], out_ref.at[0, rows], sems.at[o // 2])

    @pl.loop(0, C, step=O_BLOCK)
    def _(block_first):
        for pair in range(O_BLOCK // 2):
            o = block_first + 2 * pair
            both = jnp.concatenate(
                [
                    jnp.concatenate([spectrum_ref[o + side], bias_ref[o + side]], axis=0)
                    for side in range(2)
                ],
                axis=1,
            )
            for first in range(0, NX, X_BLOCK):
                rows = slice(first, first + X_BLOCK)
                spectral = dot(table_ref[rows, :H_ROWS], both)
                for side in range(2):
                    total = (
                        spectral[:, side * ROWS_Y : (side + 1) * ROWS_Y]
                        + skipped_ref[o + side, rows, :]
                    )
                    tile_ref[o + side, rows, :] = gelu(total).astype(BF16)
            copy_out(o).start()

    for o in range(0, C, 2):
        copy_out(o).wait()


def in_place(value):
    return pltpu.with_memory_space_constraint(value, pltpu.HBM)


def whole(shape):
    return pl.BlockSpec(shape, lambda *_: (0,) * len(shape))


def forward(field, weight):
    block = jax.ShapeDtypeStruct((4 * MODES, LANES), F32)
    share = (2, HALF_KX, KZ, C * C)
    xtable, ytable = forward_tables()
    in_hbm = pl.BlockSpec(memory_space=pltpu.HBM)
    return pl.pallas_call(
        forward_kernel,
        in_specs=[in_hbm] * 4,
        out_shape=[block] * PARTS_Y + [jax.ShapeDtypeStruct(share, F32)],
        scratch_shapes=[
            pltpu.VMEM(xtable.shape, BF16),
            pltpu.VMEM(ytable.shape[1:], BF16),
            pltpu.VMEM(share, BF16),
            pltpu.VMEM((C, NX, ROWS_Y), BF16),
            pltpu.VMEM((2 * PARTS_Y, C * KX, ROWS_Y), F32),
            pltpu.SemaphoreType.DMA((len(CHUNKS) + 3,)),
        ],
        compiler_params=pltpu.CompilerParams(vmem_limit_bytes=16 * 1024 * 1024),
        name="forward",
    )(
        in_place(field),
        in_place(jnp.asarray(xtable)),
        in_place(jnp.asarray(ytable)),
        in_place(weight),
    )


def per_device(field, spectral_weight, skip_weight, skip_bias):
    block = jax.ShapeDtypeStruct((4 * MODES, LANES), F32)
    *parts, send = forward(field, spectral_weight)
    turns = [[(i, (i + k) % PARTS_Y) for i in range(PARTS_Y)] for k in range(PARTS_Y)]
    parts = [parts[0]] + [lax.ppermute(parts[k], "gy", turns[k]) for k in ORDER]
    kron, bias_rows = prepare(skip_weight, skip_bias)
    other = lax.ppermute(send, "gz", [(i, i ^ 1) for i in range(PARTS_Z)])
    small = pltpu.CompilerParams(vmem_limit_bytes=12 * 1024 * 1024)
    sent = pl.pallas_call(
        collect_kernel,
        in_specs=[pl.BlockSpec(memory_space=pltpu.VMEM)] * PARTS_Y
        + [pl.BlockSpec(memory_space=pl.ANY)],
        out_shape=block,
        compiler_params=small,
        name="collect",
    )(*parts, kron)
    got = lax.all_to_all(sent.reshape(PARTS_Z, 2, LANES), "gz", 0, 0, tiled=True)
    mixed = pl.pallas_call(
        middle_kernel,
        out_shape=block,
        compiler_params=small,
        name="middle",
    )(got.reshape(block.shape), spectral_weight, other, jnp.asarray(middle_tables()))
    got = lax.all_to_all(mixed.reshape(PARTS_Z, 2, LANES), "gz", 0, 0, tiled=True)
    mine = got.reshape(block.shape)
    blocks = [mine] + [lax.ppermute(mine, "gy", turns[k]) for k in BACK_ORDER]
    return inverse(blocks, skip(mine, field, kron), bias_rows)


def prepare(skip_weight, skip_bias):
    return pl.pallas_call(
        prepare_kernel,
        in_specs=[
            pl.BlockSpec(memory_space=pltpu.VMEM),
            pl.BlockSpec(memory_space=pltpu.SMEM),
        ],
        out_shape=[
            jax.ShapeDtypeStruct((8 * C, 8 * C), BF16),
            jax.ShapeDtypeStruct((C, 16, ROWS_Y), BF16),
        ],
        compiler_params=pltpu.CompilerParams(vmem_limit_bytes=12 * 1024 * 1024),
        cost_estimate=pl.CostEstimate(flops=10**9, bytes_accessed=10**6, transcendentals=0),
        name="prepare",
    )(skip_weight, skip_bias)


def skip(after, field, kron):
    return pl.pallas_call(
        skip_kernel,
        in_specs=[
            pl.BlockSpec(memory_space=pl.ANY),
            pl.BlockSpec(memory_space=pltpu.VMEM),
            pl.BlockSpec(memory_space=pltpu.VMEM),
        ],
        out_shape=jax.ShapeDtypeStruct((C, NX, ROWS_Y), F32),
        compiler_params=pltpu.CompilerParams(vmem_limit_bytes=12 * 1024 * 1024),
        cost_estimate=pl.CostEstimate(flops=2 * 10**9, bytes_accessed=10**7, transcendentals=0),
        name="skip",
    )(after, field, kron)


def inverse(blocks, skipped, bias_rows):
    table = inverse_tables()
    return pl.pallas_call(
        inverse_kernel,
        out_specs=pl.BlockSpec(memory_space=pltpu.HBM),
        out_shape=jax.ShapeDtypeStruct((1, C, NX, ROWS_Y), BF16),
        scratch_shapes=[
            pltpu.VMEM((C, 2 * MODES, ROWS_Y), BF16),
            pltpu.VMEM((C, NX, ROWS_Y), BF16),
            pltpu.SemaphoreType.DMA((C // 2,)),
        ],
        compiler_params=pltpu.CompilerParams(vmem_limit_bytes=12 * 1024 * 1024),
        name="inverse",
    )(*blocks, skipped, jnp.asarray(table), bias_rows)


def solution(mesh):
    placed = (P("gz", None, None, "gy"), P(None, "gy", "gz", None), P(), P())
    return jax.shard_map(
        per_device, mesh=mesh, in_specs=placed, out_specs=P("gz", None, None, "gy"), check_vma=False
    )
```

```python
import functools
import math

import jax
import jax.numpy as jnp
import ml_dtypes
import numpy as np
from jax import lax
from jax.experimental import pallas as pl
from jax.experimental.pallas import tpu as pltpu
from jax.sharding import PartitionSpec as P

NX = 512
NY = 512
NZ = 64
C = 32
MODES = 32
PARTS_Y = 4
PARTS_Z = 64
ROWS_Y = NY // PARTS_Y
KX = MODES // PARTS_Y
HALF_KX = KX // 2
KZ = MODES * MODES // PARTS_Z
HALF = C // 2
LANES = HALF * KX
X_BLOCK = 128
O_BLOCK = 32
BACK_ORDER = (3, 1, 2)
CHUNKS = (8, 8, 8, 8)
H_ROWS = 80
F32 = jnp.float32
BF16 = jnp.bfloat16
TABLE = ml_dtypes.bfloat16


def phase_table(length):
    index = np.arange(MODES)
    freqs = np.where(index < MODES // 2, index, index - MODES)
    product = np.mod(freqs[:, None] * np.arange(length)[None, :], length)
    angle = product.astype(np.float32) * np.float32(2.0 * math.pi / length)
    return np.cos(angle).astype(np.float32), np.sin(angle).astype(np.float32)


def split_table(table):
    hi = table.astype(TABLE)
    lo = (table - hi.astype(np.float32)).astype(TABLE)
    return hi, lo


def forward_tables():
    cos_x, sin_x = phase_table(NX)
    rows = [part[g * HALF_KX : (g + 1) * HALF_KX] for g in range(2 * PARTS_Y) for part in (cos_x, -sin_x)]
    xtable = np.concatenate(rows, axis=0).astype(TABLE)
    cos_y, sin_y = phase_table(NY)
    hi, lo = split_table(np.concatenate([cos_y, sin_y], axis=0))
    both = np.concatenate([hi, lo], axis=0).reshape(4 * MODES, PARTS_Y, ROWS_Y)
    return xtable, np.ascontiguousarray(both.transpose(1, 0, 2))


def middle_tables():
    cos_z, sin_z = phase_table(NZ)
    into, back = [], []
    for h in range(2):
        order = (np.arange(MODES) + h * KZ) % MODES
        cos_h, sin_h = cos_z[order], sin_z[order]
        hi, lo = split_table(np.concatenate([cos_h, sin_h], axis=0))
        into.append(np.concatenate([hi, hi, lo], axis=1))
        hi, lo = split_table(np.concatenate([cos_h, sin_h], axis=0).T)
        back.append(np.concatenate([hi, hi, lo], axis=1))
    channel = np.arange(LANES) // KX
    spread = (channel[:, None] == np.arange(HALF * C)[None, :] // C).astype(TABLE)
    column = np.arange(2 * LANES) // KX
    gather = (np.arange(4 * C)[:, None] % C == column[None, :]).astype(TABLE)
    table = np.zeros((6 * MODES * 2, 6 * LANES), TABLE)
    table[: 2 * LANES, : 4 * LANES] = np.concatenate([spread, spread], axis=0)
    table[: 2 * LANES, 4 * LANES :] = np.concatenate([gather, gather], axis=0)
    for h in range(2):
        first = 2 * LANES + h * PARTS_Z
        table[first : first + PARTS_Z, : 3 * PARTS_Z] = into[h]
        table[first : first + PARTS_Z, 2 * LANES : 2 * LANES + 6 * MODES] = back[h]
    return table


def inverse_tables():
    cos_x, sin_x = phase_table(NX)
    rows = [part[g * HALF_KX : (g + 1) * HALF_KX] for g in range(2 * PARTS_Y) for part in (cos_x, -sin_x)]
    ones = np.zeros((H_ROWS - 2 * MODES, NX), np.float32)
    ones[:3] = 1.0
    xback = (0.5 * np.concatenate(rows + [ones], axis=0).astype(TABLE).astype(np.float32)).T
    xback = np.pad(xback, ((0, 0), (0, ROWS_Y - H_ROWS))).astype(TABLE)
    cos_y, sin_y = phase_table(NY)
    scale = np.float32(1.0 / (NX * NY * NZ))
    tables = [xback]
    for b in range(PARTS_Y):
        own = slice(b * ROWS_Y, (b + 1) * ROWS_Y)
        for part in (cos_y, sin_y):
            hi, lo = split_table(part[:, own] * scale)
            tables.append(np.concatenate([hi, hi, lo], axis=0))
    return np.concatenate(tables, axis=0)


def split(value):
    hi = value.astype(BF16)
    lo = (value - hi.astype(F32)).astype(BF16)
    return hi, lo


def turn(value, sign):
    first = lax.rem(lax.broadcasted_iota(jnp.int32, (value.shape[0], LANES), 1), KX) < HALF_KX
    parts = []
    for at in range(0, value.shape[1], LANES):
        part = value[:, at : at + LANES]
        ahead = pltpu.roll(part, LANES - HALF_KX, axis=1)
        behind = pltpu.roll(part, HALF_KX, axis=1)
        parts.append(jnp.where(first, sign * ahead, -sign * behind))
    return jnp.concatenate(parts, axis=1) if len(parts) > 1 else parts[0]


def dot(left, right, contract=((1,), (0,))):
    return lax.dot_general(left, right, (contract, ((), ())), preferred_element_type=F32)


def forward_kernel(field_ref, xtable_ref, ytable_ref, weight_ref, *refs):
    out_ref, send_ref, xrows_ref, yrows_ref, weights_ref, planes_ref, along_ref, sems = refs
    h = lax.rem(lax.axis_index("gz"), 2)
    me = lax.axis_index("gy")
    chunk_count = len(CHUNKS)
    edges = np.cumsum((0,) + CHUNKS).tolist()
    tables = [
        pltpu.make_async_copy(xtable_ref, xrows_ref, sems.at[chunk_count]),
        pltpu.make_async_copy(ytable_ref.at[me], yrows_ref, sems.at[chunk_count + 1]),
    ]
    chunks = [
        pltpu.make_async_copy(
            field_ref.at[0, pl.ds(edges[i], CHUNKS[i])],
            planes_ref.at[pl.ds(edges[i], CHUNKS[i])],
            sems.at[i],
        )
        for i in range(chunk_count)
    ]
    weights = pltpu.make_async_copy(
        weight_ref.at[:, pl.ds((1 - h) * HALF_KX, HALF_KX)], weights_ref, sems.at[chunk_count + 2]
    )
    for copy in tables + chunks[:2] + [weights] + chunks[2:]:
        copy.start()
    for copy in tables:
        copy.wait()
    xtable = xrows_ref[...]
    own = yrows_ref[...]
    table = jnp.concatenate([own, own], axis=1)
    for i in range(chunk_count):
        chunks[i].wait()
        for first in range(edges[i], edges[i + 1], 2):
            planes = jnp.concatenate([planes_ref[first], planes_ref[first + 1]], axis=1)
            along = dot(xtable, planes)
            for side in range(2):
                rows = slice((first + side) * KX, (first + side + 1) * KX)
                for group in range(2 * PARTS_Y):
                    along_ref[group, rows, :] = along[
                        group * KX : (group + 1) * KX, side * ROWS_Y : (side + 1) * ROWS_Y
                    ]
        if i == 2:
            weights.wait()
            send_ref[...] = weights_ref[...].astype(F32)
        for half, k in [
            (half, k)
            for half in range(2)
            if edges[i] < (half + 1) * HALF <= edges[i + 1]
            for k in range(PARTS_Y)
        ]:
            b = k
            for side in range(2):
                hi, lo = split(along_ref[2 * b + side, half * LANES : (half + 1) * LANES, :])
                both = jnp.concatenate([hi, lo], axis=1)
                full = dot(table, both, ((1,), (1,)))
                sums = full[: 2 * MODES] + full[2 * MODES :]
                row = (side * PARTS_Y + b) * 2 + half
                out_ref[pl.ds(row, MODES, stride=16), :] = sums[:MODES] + turn(sums[MODES:], 1.0)


def middle_kernel(recv_ref, weight_ref, other_ref, table_ref, out_ref):
    h = lax.rem(lax.axis_index("gz"), 2)
    own = pl.multiple_of(2 * LANES + h * PARTS_Z, PARTS_Z)
    into = table_ref[pl.ds(own, PARTS_Z), : 3 * PARTS_Z]
    back = table_ref[pl.ds(own, PARTS_Z), 2 * LANES : 2 * LANES + 6 * MODES]
    spread = table_ref[: 2 * LANES, : 4 * LANES]
    gather = table_ref[: 2 * LANES, 4 * LANES :]
    planes = jnp.concatenate(
        [
            sum(recv_ref[pl.ds(2 * b + half, PARTS_Z, stride=8), :] for b in range(PARTS_Y))
            for half in range(2)
        ],
        axis=1,
    )
    hi, lo = split(planes)
    sums = dot(into, jnp.concatenate([hi, lo, hi], axis=0))
    spectrum = sums[:MODES] + turn(sums[MODES:], 1.0)
    lane = lax.rem(lax.broadcasted_iota(jnp.int32, spectrum.shape, 1), KX)
    picks = [lane == at for at in range(KX)]
    rows = jnp.concatenate([jnp.where(pick, spectrum, 0.0) for pick in picks], axis=0)
    hi, lo = split(rows)
    modes = HALF_KX * MODES
    acc_r = jnp.zeros((modes, 4 * C), F32)
    acc_i = jnp.zeros((modes, 4 * C), F32)
    for half in range(2):
        cut = slice(half * LANES, (half + 1) * LANES)
        wide = dot(jnp.concatenate([hi[:, cut], lo[:, cut]], axis=1), spread)
        for block in range(4):
            lanes = slice(block * 4 * C, (block + 1) * 4 * C)
            first = half * HALF * C + block * 4 * C
            w_r, w_i = [
                jnp.concatenate(
                    [
                        weight_ref[part, pl.ds(h * HALF_KX, HALF_KX), :, first : first + 4 * C].astype(F32),
                        other_ref[part, :, :, first : first + 4 * C],
                    ],
                    axis=1,
                ).reshape(modes, 4 * C)
                for part in range(2)
            ]
            f_r, f_i = wide[:modes, lanes], wide[modes:, lanes]
            acc_r = acc_r + (f_r * w_r - f_i * w_i)
            acc_i = acc_i + (f_r * w_i + f_i * w_r)
    hi, lo = split(jnp.concatenate([acc_r, acc_i], axis=0))
    mixed = dot(jnp.concatenate([hi, lo], axis=1), gather)
    total = jnp.zeros(spectrum.shape, F32)
    for at, pick in enumerate(picks):
        total = total + jnp.where(pick, mixed[at * MODES : (at + 1) * MODES], 0.0)
    hi, lo = split(jnp.concatenate([total, turn(total, -1.0)], axis=0))
    result = dot(back, jnp.concatenate([hi, lo, hi], axis=0))
    for half in range(2):
        out_ref[pl.ds(half, PARTS_Z, stride=2), :] = result[:, half * LANES : (half + 1) * LANES]


def gelu(half):
    return half * lax.erf(half * math.sqrt(2.0)) + half


def prepare_kernel(after_ref, skip_ref, bias_ref, kron_ref, bias_rows_ref):
    del after_ref
    row = lax.broadcasted_iota(jnp.int32, (16, ROWS_Y), 0)
    for o in range(C):
        bias = jnp.full((16, ROWS_Y), bias_ref[o], F32)
        hi = bias.astype(BF16).astype(F32)
        mid = (bias - hi).astype(BF16).astype(F32)
        low = bias - hi - mid
        pieces = jnp.where(row == 0, hi, jnp.where(row == 1, mid, jnp.where(row == 2, low, 0.0)))
        bias_rows_ref[o] = pieces.astype(BF16)
    size = 8 * C
    out_row = lax.broadcasted_iota(jnp.int32, (size, C), 0)
    out_col = lax.broadcasted_iota(jnp.int32, (size, C), 1)
    rows_of = (out_row // 8 == out_col).astype(F32).astype(BF16)
    wide = dot(rows_of, skip_ref[...], ((1,), (1,))).astype(BF16)
    wide = dot(wide, rows_of, ((1,), (1,)))
    i = lax.broadcasted_iota(jnp.int32, (size, size), 0)
    j = lax.broadcasted_iota(jnp.int32, (size, size), 1)
    same = lax.rem(i, 8) == lax.rem(j, 8)
    kron_ref[...] = jnp.where(same, wide * 0.5, 0.0).astype(BF16)


def skip_kernel(after_ref, field_ref, kron_ref, out_ref):
    del after_ref
    for first in range(0, NX, 32):
        groups = []
        for at in (first, first + 16):
            wide = field_ref[0, :, at : at + 16, :].astype(F32)
            groups += [wide[:, :8].reshape(8 * C, ROWS_Y), wide[:, 8:].reshape(8 * C, ROWS_Y)]
        skipped = dot(kron_ref[...], jnp.concatenate(groups, axis=1).astype(BF16))
        for g in range(4):
            out_ref[:, first + 8 * g : first + 8 * (g + 1), :] = skipped[
                :, g * ROWS_Y : (g + 1) * ROWS_Y
            ].reshape(C, 8, ROWS_Y)


def inverse_kernel(
    r0, r1, r2, r3, skipped_ref, table_ref, bias_ref, out_ref, spectrum_ref, tile_ref, sems
):
    me = lax.axis_index("gy")
    start = pl.multiple_of(NX + me * 6 * MODES, 6 * MODES)
    table = table_ref[pl.ds(start, 6 * MODES), :]
    for k, block in zip((0,) + BACK_ORDER, (r0, r1, r2, r3)):
        b = lax.rem(me + PARTS_Y - k, PARTS_Y)
        at = pl.multiple_of(b * 2 * KX, 2 * KX)
        value = jnp.concatenate(
            [block[pl.ds(2 * side + half, MODES, stride=4), :] for half in range(2) for side in range(2)],
            axis=1,
        )
        pieces = [split(value), split(turn(value, -1.0))]
        rows = jnp.concatenate([v for hi, lo in pieces for v in (hi, lo, hi)], axis=0)
        full = dot(rows, table, ((0,), (0,)))
        for o in range(C):
            first = o // HALF * 2 * LANES + o % HALF * KX
            spectrum_ref[o, pl.ds(at, 2 * KX), :] = jnp.concatenate(
                [full[first : first + KX], full[first + LANES : first + LANES + KX]], axis=0
            ).astype(BF16)

    def copy_out(o):
        rows = pl.ds(o, 2)
        return pltpu.make_async_copy(tile_ref.at[rows], out_ref.at[0, rows], sems.at[o // 2])

    @pl.loop(0, C, step=O_BLOCK)
    def _(block_first):
        for pair in range(O_BLOCK // 2):
            o = block_first + 2 * pair
            both = jnp.concatenate(
                [
                    jnp.concatenate([spectrum_ref[o + side], bias_ref[o + side]], axis=0)
                    for side in range(2)
                ],
                axis=1,
            )
            for first in range(0, NX, X_BLOCK):
                rows = slice(first, first + X_BLOCK)
                spectral = dot(table_ref[rows, :H_ROWS], both)
                for side in range(2):
                    total = (
                        spectral[:, side * ROWS_Y : (side + 1) * ROWS_Y]
                        + skipped_ref[o + side, rows, :]
                    )
                    tile_ref[o + side, rows, :] = gelu(total).astype(BF16)
            copy_out(o).start()

    for o in range(0, C, 2):
        copy_out(o).wait()


def in_place(value):
    return pltpu.with_memory_space_constraint(value, pltpu.HBM)


def whole(shape):
    return pl.BlockSpec(shape, lambda *_: (0,) * len(shape))


def forward(field, weight):
    block = jax.ShapeDtypeStruct((4 * MODES, LANES), F32)
    share = (2, HALF_KX, KZ, C * C)
    xtable, ytable = forward_tables()
    in_hbm = pl.BlockSpec(memory_space=pltpu.HBM)
    return pl.pallas_call(
        forward_kernel,
        in_specs=[in_hbm] * 4,
        out_shape=[
            jax.ShapeDtypeStruct((PARTS_Y * block.shape[0], LANES), F32),
            jax.ShapeDtypeStruct(share, F32),
        ],
        scratch_shapes=[
            pltpu.VMEM(xtable.shape, BF16),
            pltpu.VMEM(ytable.shape[1:], BF16),
            pltpu.VMEM(share, BF16),
            pltpu.VMEM((C, NX, ROWS_Y), BF16),
            pltpu.VMEM((2 * PARTS_Y, C * KX, ROWS_Y), F32),
            pltpu.SemaphoreType.DMA((len(CHUNKS) + 3,)),
        ],
        compiler_params=pltpu.CompilerParams(vmem_limit_bytes=16 * 1024 * 1024),
        name="forward",
    )(
        in_place(field),
        in_place(jnp.asarray(xtable)),
        in_place(jnp.asarray(ytable)),
        in_place(weight),
    )


def per_device(field, spectral_weight, skip_weight, skip_bias):
    block = jax.ShapeDtypeStruct((4 * MODES, LANES), F32)
    parts, send = forward(field, spectral_weight)
    turns = [[(i, (i + k) % PARTS_Y) for i in range(PARTS_Y)] for k in range(PARTS_Y)]
    other = lax.ppermute(send, "gz", [(i, i ^ 1) for i in range(PARTS_Z)])
    small = pltpu.CompilerParams(vmem_limit_bytes=12 * 1024 * 1024)
    got = parts.reshape(PARTS_Z * PARTS_Y, 2, LANES)
    got = lax.all_to_all(got, ("gz", "gy"), 0, 0, tiled=True)
    mixed = pl.pallas_call(
        middle_kernel,
        out_shape=block,
        compiler_params=small,
        name="middle",
    )(got.reshape(PARTS_Y * block.shape[0], LANES), spectral_weight, other, jnp.asarray(middle_tables()))
    got = lax.all_to_all(mixed.reshape(PARTS_Z, 2, LANES), "gz", 0, 0, tiled=True)
    mine = got.reshape(block.shape)
    blocks = [mine] + [lax.ppermute(mine, "gy", turns[k]) for k in BACK_ORDER]
    kron, bias_rows = prepare(mine, skip_weight, skip_bias)
    return inverse(blocks, skip(mine, field, kron), bias_rows)


def prepare(after, skip_weight, skip_bias):
    return pl.pallas_call(
        prepare_kernel,
        in_specs=[
            pl.BlockSpec(memory_space=pl.ANY),
            pl.BlockSpec(memory_space=pltpu.VMEM),
            pl.BlockSpec(memory_space=pltpu.SMEM),
        ],
        out_shape=[
            jax.ShapeDtypeStruct((8 * C, 8 * C), BF16),
            jax.ShapeDtypeStruct((C, 16, ROWS_Y), BF16),
        ],
        compiler_params=pltpu.CompilerParams(vmem_limit_bytes=12 * 1024 * 1024),
        cost_estimate=pl.CostEstimate(flops=10**9, bytes_accessed=10**6, transcendentals=0),
        name="prepare",
    )(after, skip_weight, skip_bias)


def skip(after, field, kron):
    return pl.pallas_call(
        skip_kernel,
        in_specs=[
            pl.BlockSpec(memory_space=pl.ANY),
            pl.BlockSpec(memory_space=pltpu.VMEM),
            pl.BlockSpec(memory_space=pltpu.VMEM),
        ],
        out_shape=jax.ShapeDtypeStruct((C, NX, ROWS_Y), F32),
        compiler_params=pltpu.CompilerParams(vmem_limit_bytes=12 * 1024 * 1024),
        cost_estimate=pl.CostEstimate(flops=2 * 10**9, bytes_accessed=10**7, transcendentals=0),
        name="skip",
    )(after, field, kron)


def inverse(blocks, skipped, bias_rows):
    table = inverse_tables()
    return pl.pallas_call(
        inverse_kernel,
        out_specs=pl.BlockSpec(memory_space=pltpu.HBM),
        out_shape=jax.ShapeDtypeStruct((1, C, NX, ROWS_Y), BF16),
        scratch_shapes=[
            pltpu.VMEM((C, 2 * MODES, ROWS_Y), BF16),
            pltpu.VMEM((C, NX, ROWS_Y), BF16),
            pltpu.SemaphoreType.DMA((C // 2,)),
        ],
        compiler_params=pltpu.CompilerParams(vmem_limit_bytes=12 * 1024 * 1024),
        name="inverse",
    )(*blocks, skipped, jnp.asarray(table), bias_rows)


def solution(mesh):
    placed = (P("gz", None, None, "gy"), P(None, "gy", "gz", None), P(), P())
    return jax.shard_map(
        per_device, mesh=mesh, in_specs=placed, out_specs=P("gz", None, None, "gy"), check_vma=False
    )
```

```python
import functools
import math

import jax
import jax.numpy as jnp
import ml_dtypes
import numpy as np
from jax import lax
from jax.experimental import pallas as pl
from jax.experimental.pallas import tpu as pltpu
from jax.sharding import PartitionSpec as P

NX = 512
NY = 512
NZ = 64
C = 32
MODES = 32
PARTS_Y = 4
PARTS_Z = 64
ROWS_Y = NY // PARTS_Y
KX = MODES // PARTS_Y
HALF_KX = KX // 2
KZ = MODES * MODES // PARTS_Z
HALF = C // 2
LANES = HALF * KX
X_BLOCK = 128
O_BLOCK = 32
BACK_ORDER = (3, 1, 2)
CHUNKS = (8, 8, 8, 8)
H_ROWS = 80
F32 = jnp.float32
BF16 = jnp.bfloat16
TABLE = ml_dtypes.bfloat16


def phase_table(length):
    index = np.arange(MODES)
    freqs = np.where(index < MODES // 2, index, index - MODES)
    product = np.mod(freqs[:, None] * np.arange(length)[None, :], length)
    angle = product.astype(np.float32) * np.float32(2.0 * math.pi / length)
    return np.cos(angle).astype(np.float32), np.sin(angle).astype(np.float32)


def split_table(table):
    hi = table.astype(TABLE)
    lo = (table - hi.astype(np.float32)).astype(TABLE)
    return hi, lo


def forward_tables():
    cos_x, sin_x = phase_table(NX)
    rows = [part[g * HALF_KX : (g + 1) * HALF_KX] for g in range(2 * PARTS_Y) for part in (cos_x, -sin_x)]
    xtable = np.concatenate(rows, axis=0).astype(TABLE)
    cos_y, sin_y = phase_table(NY)
    hi, lo = split_table(np.concatenate([cos_y, sin_y], axis=0))
    both = np.concatenate([hi, lo], axis=0).reshape(4 * MODES, PARTS_Y, ROWS_Y)
    return xtable, np.ascontiguousarray(both.transpose(1, 0, 2))


def middle_tables():
    cos_z, sin_z = phase_table(NZ)
    into, back = [], []
    for h in range(2):
        order = (np.arange(MODES) + h * KZ) % MODES
        cos_h, sin_h = cos_z[order], sin_z[order]
        hi, lo = split_table(np.concatenate([cos_h, sin_h], axis=0))
        into.append(np.concatenate([hi, hi, lo], axis=1))
        hi, lo = split_table(np.concatenate([cos_h, sin_h], axis=0).T)
        back.append(np.concatenate([hi, hi, lo], axis=1))
    channel = np.arange(LANES) // KX
    spread = (channel[:, None] == np.arange(HALF * C)[None, :] // C).astype(TABLE)
    column = np.arange(2 * LANES) // KX
    gather = (np.arange(4 * C)[:, None] % C == column[None, :]).astype(TABLE)
    table = np.zeros((6 * MODES * 2, 6 * LANES), TABLE)
    table[: 2 * LANES, : 4 * LANES] = np.concatenate([spread, spread], axis=0)
    table[: 2 * LANES, 4 * LANES :] = np.concatenate([gather, gather], axis=0)
    for h in range(2):
        first = 2 * LANES + h * PARTS_Z
        table[first : first + PARTS_Z, : 3 * PARTS_Z] = into[h]
        table[first : first + PARTS_Z, 2 * LANES : 2 * LANES + 6 * MODES] = back[h]
    return table


def inverse_tables():
    cos_x, sin_x = phase_table(NX)
    rows = [part[g * HALF_KX : (g + 1) * HALF_KX] for g in range(2 * PARTS_Y) for part in (cos_x, -sin_x)]
    ones = np.zeros((H_ROWS - 2 * MODES, NX), np.float32)
    ones[:3] = 1.0
    xback = (0.5 * np.concatenate(rows + [ones], axis=0).astype(TABLE).astype(np.float32)).T
    xback = np.pad(xback, ((0, 0), (0, ROWS_Y - H_ROWS))).astype(TABLE)
    cos_y, sin_y = phase_table(NY)
    scale = np.float32(1.0 / (NX * NY * NZ))
    tables = [xback]
    for b in range(PARTS_Y):
        own = slice(b * ROWS_Y, (b + 1) * ROWS_Y)
        for part in (cos_y, sin_y):
            hi, lo = split_table(part[:, own] * scale)
            tables.append(np.concatenate([hi, hi, lo], axis=0))
    return np.concatenate(tables, axis=0)


def split(value):
    hi = value.astype(BF16)
    lo = (value - hi.astype(F32)).astype(BF16)
    return hi, lo


def turn(value, sign):
    first = lax.rem(lax.broadcasted_iota(jnp.int32, (value.shape[0], LANES), 1), KX) < HALF_KX
    parts = []
    for at in range(0, value.shape[1], LANES):
        part = value[:, at : at + LANES]
        ahead = pltpu.roll(part, LANES - HALF_KX, axis=1)
        behind = pltpu.roll(part, HALF_KX, axis=1)
        parts.append(jnp.where(first, sign * ahead, -sign * behind))
    return jnp.concatenate(parts, axis=1) if len(parts) > 1 else parts[0]


def dot(left, right, contract=((1,), (0,))):
    return lax.dot_general(left, right, (contract, ((), ())), preferred_element_type=F32)


def forward_kernel(field_ref, xtable_ref, ytable_ref, weight_ref, *refs):
    out_ref, send_ref, xrows_ref, yrows_ref, weights_ref, planes_ref, along_ref, sems = refs
    h = lax.rem(lax.axis_index("gz"), 2)
    me = lax.axis_index("gy")
    chunk_count = len(CHUNKS)
    edges = np.cumsum((0,) + CHUNKS).tolist()
    tables = [
        pltpu.make_async_copy(xtable_ref, xrows_ref, sems.at[chunk_count]),
        pltpu.make_async_copy(ytable_ref.at[me], yrows_ref, sems.at[chunk_count + 1]),
    ]
    chunks = [
        pltpu.make_async_copy(
            field_ref.at[0, pl.ds(edges[i], CHUNKS[i])],
            planes_ref.at[pl.ds(edges[i], CHUNKS[i])],
            sems.at[i],
        )
        for i in range(chunk_count)
    ]
    weights = pltpu.make_async_copy(
        weight_ref.at[:, pl.ds((1 - h) * HALF_KX, HALF_KX)], weights_ref, sems.at[chunk_count + 2]
    )
    for copy in tables + chunks[:2] + [weights] + chunks[2:]:
        copy.start()
    for copy in tables:
        copy.wait()
    xtable = xrows_ref[...]
    own = yrows_ref[...]
    table = jnp.concatenate([own, own], axis=1)
    for i in range(chunk_count):
        chunks[i].wait()
        for first in range(edges[i], edges[i + 1], 2):
            planes = jnp.concatenate([planes_ref[first], planes_ref[first + 1]], axis=1)
            along = dot(xtable, planes)
            for side in range(2):
                rows = slice((first + side) * KX, (first + side + 1) * KX)
                for group in range(2 * PARTS_Y):
                    along_ref[group, rows, :] = along[
                        group * KX : (group + 1) * KX, side * ROWS_Y : (side + 1) * ROWS_Y
                    ]
        if i == 2:
            weights.wait()
            send_ref[...] = weights_ref[...].astype(F32)
        for half, k in [
            (half, k)
            for half in range(2)
            if edges[i] < (half + 1) * HALF <= edges[i + 1]
            for k in range(PARTS_Y)
        ]:
            for side in range(2):
                hi, lo = split(along_ref[2 * k + side, half * LANES : (half + 1) * LANES, :])
                both = jnp.concatenate([hi, lo], axis=1)
                full = dot(table, both, ((1,), (1,)))
                sums = full[: 2 * MODES] + full[2 * MODES :]
                row = k * 4 * MODES + 2 * side + half
                out_ref[pl.ds(row, MODES, stride=4), :] = sums[:MODES] + turn(sums[MODES:], 1.0)


def middle_kernel(recv_ref, weight_ref, other_ref, table_ref, out_ref):
    h = lax.rem(lax.axis_index("gz"), 2)
    own = pl.multiple_of(2 * LANES + h * PARTS_Z, PARTS_Z)
    into = table_ref[pl.ds(own, PARTS_Z), : 3 * PARTS_Z]
    back = table_ref[pl.ds(own, PARTS_Z), 2 * LANES : 2 * LANES + 6 * MODES]
    spread = table_ref[: 2 * LANES, : 4 * LANES]
    gather = table_ref[: 2 * LANES, 4 * LANES :]
    planes = jnp.concatenate(
        [
            sum(recv_ref[pl.ds(b * 2 * PARTS_Z + half, PARTS_Z, stride=2), :] for b in range(PARTS_Y))
            for half in range(2)
        ],
        axis=1,
    )
    hi, lo = split(planes)
    sums = dot(into, jnp.concatenate([hi, lo, hi], axis=0))
    spectrum = sums[:MODES] + turn(sums[MODES:], 1.0)
    lane = lax.rem(lax.broadcasted_iota(jnp.int32, spectrum.shape, 1), KX)
    picks = [lane == at for at in range(KX)]
    rows = jnp.concatenate([jnp.where(pick, spectrum, 0.0) for pick in picks], axis=0)
    hi, lo = split(rows)
    modes = HALF_KX * MODES
    acc_r = jnp.zeros((modes, 4 * C), F32)
    acc_i = jnp.zeros((modes, 4 * C), F32)
    for half in range(2):
        cut = slice(half * LANES, (half + 1) * LANES)
        wide = dot(jnp.concatenate([hi[:, cut], lo[:, cut]], axis=1), spread)
        for block in range(4):
            lanes = slice(block * 4 * C, (block + 1) * 4 * C)
            first = half * HALF * C + block * 4 * C
            w_r, w_i = [
                jnp.concatenate(
                    [
                        weight_ref[part, pl.ds(h * HALF_KX, HALF_KX), :, first : first + 4 * C].astype(F32),
                        other_ref[part, :, :, first : first + 4 * C],
                    ],
                    axis=1,
                ).reshape(modes, 4 * C)
                for part in range(2)
            ]
            f_r, f_i = wide[:modes, lanes], wide[modes:, lanes]
            acc_r = acc_r + (f_r * w_r - f_i * w_i)
            acc_i = acc_i + (f_r * w_i + f_i * w_r)
    hi, lo = split(jnp.concatenate([acc_r, acc_i], axis=0))
    mixed = dot(jnp.concatenate([hi, lo], axis=1), gather)
    total = jnp.zeros(spectrum.shape, F32)
    for at, pick in enumerate(picks):
        total = total + jnp.where(pick, mixed[at * MODES : (at + 1) * MODES], 0.0)
    hi, lo = split(jnp.concatenate([total, turn(total, -1.0)], axis=0))
    result = dot(back, jnp.concatenate([hi, lo, hi], axis=0))
    for half in range(2):
        out_ref[pl.ds(half, PARTS_Z, stride=2), :] = result[:, half * LANES : (half + 1) * LANES]


def gelu(half):
    return half * lax.erf(half * math.sqrt(2.0)) + half


def prepare_kernel(after_ref, skip_ref, bias_ref, kron_ref, bias_rows_ref):
    del after_ref
    row = lax.broadcasted_iota(jnp.int32, (16, ROWS_Y), 0)
    for o in range(C):
        bias = jnp.full((16, ROWS_Y), bias_ref[o], F32)
        hi = bias.astype(BF16).astype(F32)
        mid = (bias - hi).astype(BF16).astype(F32)
        low = bias - hi - mid
        pieces = jnp.where(row == 0, hi, jnp.where(row == 1, mid, jnp.where(row == 2, low, 0.0)))
        bias_rows_ref[o] = pieces.astype(BF16)
    size = 8 * C
    out_row = lax.broadcasted_iota(jnp.int32, (size, C), 0)
    out_col = lax.broadcasted_iota(jnp.int32, (size, C), 1)
    rows_of = (out_row // 8 == out_col).astype(F32).astype(BF16)
    wide = dot(rows_of, skip_ref[...], ((1,), (1,))).astype(BF16)
    wide = dot(wide, rows_of, ((1,), (1,)))
    i = lax.broadcasted_iota(jnp.int32, (size, size), 0)
    j = lax.broadcasted_iota(jnp.int32, (size, size), 1)
    same = lax.rem(i, 8) == lax.rem(j, 8)
    kron_ref[...] = jnp.where(same, wide * 0.5, 0.0).astype(BF16)


def skip_kernel(after_ref, field_ref, kron_ref, out_ref):
    del after_ref
    for first in range(0, NX, 32):
        groups = []
        for at in (first, first + 16):
            wide = field_ref[0, :, at : at + 16, :].astype(F32)
            groups += [wide[:, :8].reshape(8 * C, ROWS_Y), wide[:, 8:].reshape(8 * C, ROWS_Y)]
        skipped = dot(kron_ref[...], jnp.concatenate(groups, axis=1).astype(BF16))
        for g in range(4):
            out_ref[:, first + 8 * g : first + 8 * (g + 1), :] = skipped[
                :, g * ROWS_Y : (g + 1) * ROWS_Y
            ].reshape(C, 8, ROWS_Y)


def inverse_kernel(
    r0, r1, r2, r3, skipped_ref, table_ref, bias_ref, out_ref, spectrum_ref, tile_ref, sems
):
    me = lax.axis_index("gy")
    start = pl.multiple_of(NX + me * 6 * MODES, 6 * MODES)
    table = table_ref[pl.ds(start, 6 * MODES), :]
    for k, block in zip((0,) + BACK_ORDER, (r0, r1, r2, r3)):
        b = lax.rem(me + PARTS_Y - k, PARTS_Y)
        at = pl.multiple_of(b * 2 * KX, 2 * KX)
        value = jnp.concatenate(
            [block[pl.ds(2 * side + half, MODES, stride=4), :] for half in range(2) for side in range(2)],
            axis=1,
        )
        pieces = [split(value), split(turn(value, -1.0))]
        rows = jnp.concatenate([v for hi, lo in pieces for v in (hi, lo, hi)], axis=0)
        full = dot(rows, table, ((0,), (0,)))
        for o in range(C):
            first = o // HALF * 2 * LANES + o % HALF * KX
            spectrum_ref[o, pl.ds(at, 2 * KX), :] = jnp.concatenate(
                [full[first : first + KX], full[first + LANES : first + LANES + KX]], axis=0
            ).astype(BF16)

    def copy_out(o):
        rows = pl.ds(o, 2)
        return pltpu.make_async_copy(tile_ref.at[rows], out_ref.at[0, rows], sems.at[o // 2])

    @pl.loop(0, C, step=O_BLOCK)
    def _(block_first):
        for pair in range(O_BLOCK // 2):
            o = block_first + 2 * pair
            both = jnp.concatenate(
                [
                    jnp.concatenate([spectrum_ref[o + side], bias_ref[o + side]], axis=0)
                    for side in range(2)
                ],
                axis=1,
            )
            for first in range(0, NX, X_BLOCK):
                rows = slice(first, first + X_BLOCK)
                spectral = dot(table_ref[rows, :H_ROWS], both)
                for side in range(2):
                    total = (
                        spectral[:, side * ROWS_Y : (side + 1) * ROWS_Y]
                        + skipped_ref[o + side, rows, :]
                    )
                    tile_ref[o + side, rows, :] = gelu(total).astype(BF16)
            copy_out(o).start()

    for o in range(0, C, 2):
        copy_out(o).wait()


def in_place(value):
    return pltpu.with_memory_space_constraint(value, pltpu.HBM)


def whole(shape):
    return pl.BlockSpec(shape, lambda *_: (0,) * len(shape))


def forward(field, weight):
    block = jax.ShapeDtypeStruct((4 * MODES, LANES), F32)
    share = (2, HALF_KX, KZ, C * C)
    xtable, ytable = forward_tables()
    in_hbm = pl.BlockSpec(memory_space=pltpu.HBM)
    return pl.pallas_call(
        forward_kernel,
        in_specs=[in_hbm] * 4,
        out_shape=[
            jax.ShapeDtypeStruct((PARTS_Y * block.shape[0], LANES), F32),
            jax.ShapeDtypeStruct(share, F32),
        ],
        scratch_shapes=[
            pltpu.VMEM(xtable.shape, BF16),
            pltpu.VMEM(ytable.shape[1:], BF16),
            pltpu.VMEM(share, BF16),
            pltpu.VMEM((C, NX, ROWS_Y), BF16),
            pltpu.VMEM((2 * PARTS_Y, C * KX, ROWS_Y), F32),
            pltpu.SemaphoreType.DMA((len(CHUNKS) + 3,)),
        ],
        compiler_params=pltpu.CompilerParams(vmem_limit_bytes=16 * 1024 * 1024),
        name="forward",
    )(
        in_place(field),
        in_place(jnp.asarray(xtable)),
        in_place(jnp.asarray(ytable)),
        in_place(weight),
    )


def per_device(field, spectral_weight, skip_weight, skip_bias):
    block = jax.ShapeDtypeStruct((4 * MODES, LANES), F32)
    parts, send = forward(field, spectral_weight)
    turns = [[(i, (i + k) % PARTS_Y) for i in range(PARTS_Y)] for k in range(PARTS_Y)]
    other = lax.ppermute(send, "gz", [(i, i ^ 1) for i in range(PARTS_Z)])
    small = pltpu.CompilerParams(vmem_limit_bytes=12 * 1024 * 1024)
    got = parts.reshape(PARTS_Z * PARTS_Y, 2, LANES)
    got = lax.all_to_all(got, ("gy", "gz"), 0, 0, tiled=True)
    mixed = pl.pallas_call(
        middle_kernel,
        out_shape=block,
        compiler_params=small,
        name="middle",
    )(got.reshape(PARTS_Y * block.shape[0], LANES), spectral_weight, other, jnp.asarray(middle_tables()))
    got = lax.all_to_all(mixed.reshape(PARTS_Z, 2, LANES), "gz", 0, 0, tiled=True)
    mine = got.reshape(block.shape)
    blocks = [mine] + [lax.ppermute(mine, "gy", turns[k]) for k in BACK_ORDER]
    kron, bias_rows = prepare(mine, skip_weight, skip_bias)
    return inverse(blocks, skip(mine, field, kron), bias_rows)


def prepare(after, skip_weight, skip_bias):
    return pl.pallas_call(
        prepare_kernel,
        in_specs=[
            pl.BlockSpec(memory_space=pl.ANY),
            pl.BlockSpec(memory_space=pltpu.VMEM),
            pl.BlockSpec(memory_space=pltpu.SMEM),
        ],
        out_shape=[
            jax.ShapeDtypeStruct((8 * C, 8 * C), BF16),
            jax.ShapeDtypeStruct((C, 16, ROWS_Y), BF16),
        ],
        compiler_params=pltpu.CompilerParams(vmem_limit_bytes=12 * 1024 * 1024),
        cost_estimate=pl.CostEstimate(flops=10**9, bytes_accessed=10**6, transcendentals=0),
        name="prepare",
    )(after, skip_weight, skip_bias)


def skip(after, field, kron):
    return pl.pallas_call(
        skip_kernel,
        in_specs=[
            pl.BlockSpec(memory_space=pl.ANY),
            pl.BlockSpec(memory_space=pltpu.VMEM),
            pl.BlockSpec(memory_space=pltpu.VMEM),
        ],
        out_shape=jax.ShapeDtypeStruct((C, NX, ROWS_Y), F32),
        compiler_params=pltpu.CompilerParams(vmem_limit_bytes=12 * 1024 * 1024),
        cost_estimate=pl.CostEstimate(flops=2 * 10**9, bytes_accessed=10**7, transcendentals=0),
        name="skip",
    )(after, field, kron)


def inverse(blocks, skipped, bias_rows):
    table = inverse_tables()
    return pl.pallas_call(
        inverse_kernel,
        out_specs=pl.BlockSpec(memory_space=pltpu.HBM),
        out_shape=jax.ShapeDtypeStruct((1, C, NX, ROWS_Y), BF16),
        scratch_shapes=[
            pltpu.VMEM((C, 2 * MODES, ROWS_Y), BF16),
            pltpu.VMEM((C, NX, ROWS_Y), BF16),
            pltpu.SemaphoreType.DMA((C // 2,)),
        ],
        compiler_params=pltpu.CompilerParams(vmem_limit_bytes=12 * 1024 * 1024),
        name="inverse",
    )(*blocks, skipped, jnp.asarray(table), bias_rows)


def solution(mesh):
    placed = (P("gz", None, None, "gy"), P(None, "gy", "gz", None), P(), P())
    return jax.shard_map(
        per_device, mesh=mesh, in_specs=placed, out_specs=P("gz", None, None, "gy"), check_vma=False
    )
```

```python
import functools
import math

import jax
import jax.numpy as jnp
import ml_dtypes
import numpy as np
from jax import lax
from jax.experimental import pallas as pl
from jax.experimental.pallas import tpu as pltpu
from jax.sharding import PartitionSpec as P

NX = 512
NY = 512
NZ = 64
C = 32
MODES = 32
PARTS_Y = 4
PARTS_Z = 64
ROWS_Y = NY // PARTS_Y
KX = MODES // PARTS_Y
HALF_KX = KX // 2
KZ = MODES * MODES // PARTS_Z
HALF = C // 2
LANES = HALF * KX
X_BLOCK = 128
O_BLOCK = 32
BACK_ORDER = (3, 1, 2)
CHUNKS = (8, 8, 8, 8)
H_ROWS = 80
F32 = jnp.float32
BF16 = jnp.bfloat16
TABLE = ml_dtypes.bfloat16


def phase_table(length):
    index = np.arange(MODES)
    freqs = np.where(index < MODES // 2, index, index - MODES)
    product = np.mod(freqs[:, None] * np.arange(length)[None, :], length)
    angle = product.astype(np.float32) * np.float32(2.0 * math.pi / length)
    return np.cos(angle).astype(np.float32), np.sin(angle).astype(np.float32)


def split_table(table):
    hi = table.astype(TABLE)
    lo = (table - hi.astype(np.float32)).astype(TABLE)
    return hi, lo


def forward_tables():
    cos_x, sin_x = phase_table(NX)
    rows = [part[g * HALF_KX : (g + 1) * HALF_KX] for g in range(2 * PARTS_Y) for part in (cos_x, -sin_x)]
    xtable = np.concatenate(rows, axis=0).astype(TABLE)
    cos_y, sin_y = phase_table(NY)
    hi, lo = split_table(np.concatenate([cos_y, sin_y], axis=0))
    both = np.concatenate([hi, lo], axis=0).reshape(4 * MODES, PARTS_Y, ROWS_Y)
    return xtable, np.ascontiguousarray(both.transpose(1, 0, 2))


def middle_tables():
    cos_z, sin_z = phase_table(NZ)
    into, back = [], []
    for h in range(2):
        order = (np.arange(MODES) + h * KZ) % MODES
        cos_h, sin_h = cos_z[order], sin_z[order]
        hi, lo = split_table(np.concatenate([cos_h, sin_h], axis=0))
        into.append(np.concatenate([hi, hi, lo], axis=1))
        hi, lo = split_table(np.concatenate([cos_h, sin_h], axis=0).T)
        back.append(np.concatenate([hi, hi, lo], axis=1))
    channel = np.arange(LANES) // KX
    spread = (channel[:, None] == np.arange(HALF * C)[None, :] // C).astype(TABLE)
    column = np.arange(2 * LANES) // KX
    gather = (np.arange(4 * C)[:, None] % C == column[None, :]).astype(TABLE)
    table = np.zeros((6 * MODES * 2, 6 * LANES), TABLE)
    table[: 2 * LANES, : 4 * LANES] = np.concatenate([spread, spread], axis=0)
    table[: 2 * LANES, 4 * LANES :] = np.concatenate([gather, gather], axis=0)
    for h in range(2):
        first = 2 * LANES + h * PARTS_Z
        table[first : first + PARTS_Z, : 3 * PARTS_Z] = into[h]
        table[first : first + PARTS_Z, 2 * LANES : 2 * LANES + 6 * MODES] = back[h]
    return table


def inverse_tables():
    cos_x, sin_x = phase_table(NX)
    rows = [part[g * HALF_KX : (g + 1) * HALF_KX] for g in range(2 * PARTS_Y) for part in (cos_x, -sin_x)]
    ones = np.zeros((H_ROWS - 2 * MODES, NX), np.float32)
    ones[:3] = 1.0
    xback = (0.5 * np.concatenate(rows + [ones], axis=0).astype(TABLE).astype(np.float32)).T
    xback = np.pad(xback, ((0, 0), (0, ROWS_Y - H_ROWS))).astype(TABLE)
    cos_y, sin_y = phase_table(NY)
    scale = np.float32(1.0 / (NX * NY * NZ))
    tables = [xback]
    for b in range(PARTS_Y):
        own = slice(b * ROWS_Y, (b + 1) * ROWS_Y)
        for part in (cos_y, sin_y):
            hi, lo = split_table(part[:, own] * scale)
            tables.append(np.concatenate([hi, hi, lo], axis=0))
    return np.concatenate(tables, axis=0)


def split(value):
    hi = value.astype(BF16)
    lo = (value - hi.astype(F32)).astype(BF16)
    return hi, lo


def turn(value, sign):
    first = lax.rem(lax.broadcasted_iota(jnp.int32, (value.shape[0], LANES), 1), KX) < HALF_KX
    parts = []
    for at in range(0, value.shape[1], LANES):
        part = value[:, at : at + LANES]
        ahead = pltpu.roll(part, LANES - HALF_KX, axis=1)
        behind = pltpu.roll(part, HALF_KX, axis=1)
        parts.append(jnp.where(first, sign * ahead, -sign * behind))
    return jnp.concatenate(parts, axis=1) if len(parts) > 1 else parts[0]


def dot(left, right, contract=((1,), (0,))):
    return lax.dot_general(left, right, (contract, ((), ())), preferred_element_type=F32)


def forward_kernel(field_ref, xtable_ref, ytable_ref, weight_ref, *refs):
    out_ref, send_ref, xrows_ref, yrows_ref, weights_ref, planes_ref, along_ref, sems = refs
    h = lax.rem(lax.axis_index("gz"), 2)
    me = lax.axis_index("gy")
    chunk_count = len(CHUNKS)
    edges = np.cumsum((0,) + CHUNKS).tolist()
    tables = [
        pltpu.make_async_copy(xtable_ref, xrows_ref, sems.at[chunk_count]),
        pltpu.make_async_copy(ytable_ref.at[me], yrows_ref, sems.at[chunk_count + 1]),
    ]
    chunks = [
        pltpu.make_async_copy(
            field_ref.at[0, pl.ds(edges[i], CHUNKS[i])],
            planes_ref.at[pl.ds(edges[i], CHUNKS[i])],
            sems.at[i],
        )
        for i in range(chunk_count)
    ]
    weights = pltpu.make_async_copy(
        weight_ref.at[:, pl.ds((1 - h) * HALF_KX, HALF_KX)], weights_ref, sems.at[chunk_count + 2]
    )
    for copy in tables + chunks[:2] + [weights] + chunks[2:]:
        copy.start()
    for copy in tables:
        copy.wait()
    xtable = xrows_ref[...]
    own = yrows_ref[...]
    table = jnp.concatenate([own, own], axis=1)
    for i in range(chunk_count):
        chunks[i].wait()
        for first in range(edges[i], edges[i + 1], 2):
            planes = jnp.concatenate([planes_ref[first], planes_ref[first + 1]], axis=1)
            along = dot(xtable, planes)
            for side in range(2):
                rows = slice((first + side) * KX, (first + side + 1) * KX)
                for group in range(2 * PARTS_Y):
                    along_ref[group, rows, :] = along[
                        group * KX : (group + 1) * KX, side * ROWS_Y : (side + 1) * ROWS_Y
                    ]
        if i == 2:
            weights.wait()
            send_ref[...] = weights_ref[...].astype(F32)
        for half, k in [
            (half, k)
            for half in range(2)
            if edges[i] < (half + 1) * HALF <= edges[i + 1]
            for k in range(PARTS_Y)
        ]:
            for side in range(2):
                hi, lo = split(along_ref[2 * k + side, half * LANES : (half + 1) * LANES, :])
                both = jnp.concatenate([hi, lo], axis=1)
                full = dot(table, both, ((1,), (1,)))
                sums = full[: 2 * MODES] + full[2 * MODES :]
                row = k * 4 * MODES + 2 * side + half
                out_ref[pl.ds(row, MODES, stride=4), :] = sums[:MODES] + turn(sums[MODES:], 1.0)


def middle_kernel(recv_ref, weight_ref, other_ref, table_ref, out_ref):
    h = lax.rem(lax.axis_index("gz"), 2)
    own = pl.multiple_of(2 * LANES + h * PARTS_Z, PARTS_Z)
    into = table_ref[pl.ds(own, PARTS_Z), : 3 * PARTS_Z]
    back = table_ref[pl.ds(own, PARTS_Z), 2 * LANES : 2 * LANES + 6 * MODES]
    spread = table_ref[: 2 * LANES, : 4 * LANES]
    gather = table_ref[: 2 * LANES, 4 * LANES :]
    planes = jnp.concatenate(
        [
            sum(recv_ref[pl.ds(b * 2 * PARTS_Z + half, PARTS_Z, stride=2), :] for b in range(PARTS_Y))
            for half in range(2)
        ],
        axis=1,
    )
    hi, lo = split(planes)
    sums = dot(into, jnp.concatenate([hi, lo, hi], axis=0))
    spectrum = sums[:MODES] + turn(sums[MODES:], 1.0)
    lane = lax.rem(lax.broadcasted_iota(jnp.int32, spectrum.shape, 1), KX)
    picks = [lane == at for at in range(KX)]
    rows = jnp.concatenate([jnp.where(pick, spectrum, 0.0) for pick in picks], axis=0)
    hi, lo = split(rows)
    modes = HALF_KX * MODES
    acc_r = jnp.zeros((modes, 4 * C), F32)
    acc_i = jnp.zeros((modes, 4 * C), F32)
    for half in range(2):
        cut = slice(half * LANES, (half + 1) * LANES)
        wide = dot(jnp.concatenate([hi[:, cut], lo[:, cut]], axis=1), spread)
        for block in range(4):
            lanes = slice(block * 4 * C, (block + 1) * 4 * C)
            first = half * HALF * C + block * 4 * C
            w_r, w_i = [
                jnp.concatenate(
                    [
                        weight_ref[part, pl.ds(h * HALF_KX, HALF_KX), :, first : first + 4 * C].astype(F32),
                        other_ref[part, :, :, first : first + 4 * C],
                    ],
                    axis=1,
                ).reshape(modes, 4 * C)
                for part in range(2)
            ]
            f_r, f_i = wide[:modes, lanes], wide[modes:, lanes]
            acc_r = acc_r + (f_r * w_r - f_i * w_i)
            acc_i = acc_i + (f_r * w_i + f_i * w_r)
    hi, lo = split(jnp.concatenate([acc_r, acc_i], axis=0))
    mixed = dot(jnp.concatenate([hi, lo], axis=1), gather)
    total = jnp.zeros(spectrum.shape, F32)
    for at, pick in enumerate(picks):
        total = total + jnp.where(pick, mixed[at * MODES : (at + 1) * MODES], 0.0)
    hi, lo = split(jnp.concatenate([total, turn(total, -1.0)], axis=0))
    result = dot(back, jnp.concatenate([hi, lo, hi], axis=0))
    for half in range(2):
        out_ref[pl.ds(half, PARTS_Z, stride=2), :] = result[:, half * LANES : (half + 1) * LANES]


def gelu(half):
    return half * lax.erf(half * math.sqrt(2.0)) + half


def skip_kernel(after_ref, field_ref, skip_ref, bias_ref, out_ref, bias_rows_ref):
    del after_ref
    row = lax.broadcasted_iota(jnp.int32, (16, ROWS_Y), 0)
    for o in range(C):
        bias = jnp.full((16, ROWS_Y), bias_ref[o], F32)
        hi = bias.astype(BF16).astype(F32)
        mid = (bias - hi).astype(BF16).astype(F32)
        low = bias - hi - mid
        pieces = jnp.where(row == 0, hi, jnp.where(row == 1, mid, jnp.where(row == 2, low, 0.0)))
        bias_rows_ref[o] = pieces.astype(BF16)
    size = 8 * C
    out_row = lax.broadcasted_iota(jnp.int32, (size, C), 0)
    out_col = lax.broadcasted_iota(jnp.int32, (size, C), 1)
    rows_of = (out_row // 8 == out_col).astype(F32).astype(BF16)
    wide = dot(rows_of, skip_ref[...], ((1,), (1,))).astype(BF16)
    wide = dot(wide, rows_of, ((1,), (1,)))
    i = lax.broadcasted_iota(jnp.int32, (size, size), 0)
    j = lax.broadcasted_iota(jnp.int32, (size, size), 1)
    same = lax.rem(i, 8) == lax.rem(j, 8)
    kron = jnp.where(same, wide * 0.5, 0.0).astype(BF16)
    for first in range(0, NX, 32):
        groups = []
        for at in (first, first + 16):
            wide = field_ref[0, :, at : at + 16, :].astype(F32)
            groups += [wide[:, :8].reshape(8 * C, ROWS_Y), wide[:, 8:].reshape(8 * C, ROWS_Y)]
        skipped = dot(kron, jnp.concatenate(groups, axis=1).astype(BF16))
        for g in range(4):
            out_ref[:, first + 8 * g : first + 8 * (g + 1), :] = skipped[
                :, g * ROWS_Y : (g + 1) * ROWS_Y
            ].reshape(C, 8, ROWS_Y)


def inverse_kernel(
    r0, r1, r2, r3, skipped_ref, table_ref, bias_ref, out_ref, spectrum_ref, tile_ref, sems
):
    me = lax.axis_index("gy")
    start = pl.multiple_of(NX + me * 6 * MODES, 6 * MODES)
    table = table_ref[pl.ds(start, 6 * MODES), :]
    for k, block in zip((0,) + BACK_ORDER, (r0, r1, r2, r3)):
        b = lax.rem(me + PARTS_Y - k, PARTS_Y)
        at = pl.multiple_of(b * 2 * KX, 2 * KX)
        value = jnp.concatenate(
            [block[pl.ds(2 * side + half, MODES, stride=4), :] for half in range(2) for side in range(2)],
            axis=1,
        )
        pieces = [split(value), split(turn(value, -1.0))]
        rows = jnp.concatenate([v for hi, lo in pieces for v in (hi, lo, hi)], axis=0)
        full = dot(rows, table, ((0,), (0,)))
        for o in range(C):
            first = o // HALF * 2 * LANES + o % HALF * KX
            spectrum_ref[o, pl.ds(at, 2 * KX), :] = jnp.concatenate(
                [full[first : first + KX], full[first + LANES : first + LANES + KX]], axis=0
            ).astype(BF16)

    def copy_out(o):
        rows = pl.ds(o, 2)
        return pltpu.make_async_copy(tile_ref.at[rows], out_ref.at[0, rows], sems.at[o // 2])

    @pl.loop(0, C, step=O_BLOCK)
    def _(block_first):
        for pair in range(O_BLOCK // 2):
            o = block_first + 2 * pair
            both = jnp.concatenate(
                [
                    jnp.concatenate([spectrum_ref[o + side], bias_ref[o + side]], axis=0)
                    for side in range(2)
                ],
                axis=1,
            )
            for first in range(0, NX, X_BLOCK):
                rows = slice(first, first + X_BLOCK)
                spectral = dot(table_ref[rows, :H_ROWS], both)
                for side in range(2):
                    total = (
                        spectral[:, side * ROWS_Y : (side + 1) * ROWS_Y]
                        + skipped_ref[o + side, rows, :]
                    )
                    tile_ref[o + side, rows, :] = gelu(total).astype(BF16)
            copy_out(o).start()

    for o in range(0, C, 2):
        copy_out(o).wait()


def in_place(value):
    return pltpu.with_memory_space_constraint(value, pltpu.HBM)


def whole(shape):
    return pl.BlockSpec(shape, lambda *_: (0,) * len(shape))


def forward(field, weight):
    block = jax.ShapeDtypeStruct((4 * MODES, LANES), F32)
    share = (2, HALF_KX, KZ, C * C)
    xtable, ytable = forward_tables()
    in_hbm = pl.BlockSpec(memory_space=pltpu.HBM)
    return pl.pallas_call(
        forward_kernel,
        in_specs=[in_hbm] * 4,
        out_shape=[
            jax.ShapeDtypeStruct((PARTS_Y * block.shape[0], LANES), F32),
            jax.ShapeDtypeStruct(share, F32),
        ],
        scratch_shapes=[
            pltpu.VMEM(xtable.shape, BF16),
            pltpu.VMEM(ytable.shape[1:], BF16),
            pltpu.VMEM(share, BF16),
            pltpu.VMEM((C, NX, ROWS_Y), BF16),
            pltpu.VMEM((2 * PARTS_Y, C * KX, ROWS_Y), F32),
            pltpu.SemaphoreType.DMA((len(CHUNKS) + 3,)),
        ],
        compiler_params=pltpu.CompilerParams(vmem_limit_bytes=16 * 1024 * 1024),
        name="forward",
    )(
        in_place(field),
        in_place(jnp.asarray(xtable)),
        in_place(jnp.asarray(ytable)),
        in_place(weight),
    )


def per_device(field, spectral_weight, skip_weight, skip_bias):
    block = jax.ShapeDtypeStruct((4 * MODES, LANES), F32)
    parts, send = forward(field, spectral_weight)
    turns = [[(i, (i + k) % PARTS_Y) for i in range(PARTS_Y)] for k in range(PARTS_Y)]
    other = lax.ppermute(send, "gz", [(i, i ^ 1) for i in range(PARTS_Z)])
    small = pltpu.CompilerParams(vmem_limit_bytes=12 * 1024 * 1024)
    got = parts.reshape(PARTS_Z * PARTS_Y, 2, LANES)
    got = lax.all_to_all(got, ("gy", "gz"), 0, 0, tiled=True)
    mixed = pl.pallas_call(
        middle_kernel,
        out_shape=block,
        compiler_params=small,
        name="middle",
    )(got.reshape(PARTS_Y * block.shape[0], LANES), spectral_weight, other, jnp.asarray(middle_tables()))
    got = lax.all_to_all(mixed.reshape(PARTS_Z, 2, LANES), "gz", 0, 0, tiled=True)
    mine = got.reshape(block.shape)
    blocks = [mine] + [lax.ppermute(mine, "gy", turns[k]) for k in BACK_ORDER]
    skipped, bias_rows = skip(mine, field, skip_weight, skip_bias)
    return inverse(blocks, skipped, bias_rows)


def skip(after, field, skip_weight, skip_bias):
    return pl.pallas_call(
        skip_kernel,
        in_specs=[
            pl.BlockSpec(memory_space=pl.ANY),
            pl.BlockSpec(memory_space=pltpu.VMEM),
            pl.BlockSpec(memory_space=pltpu.VMEM),
            pl.BlockSpec(memory_space=pltpu.SMEM),
        ],
        out_shape=[
            jax.ShapeDtypeStruct((C, NX, ROWS_Y), F32),
            jax.ShapeDtypeStruct((C, 16, ROWS_Y), BF16),
        ],
        compiler_params=pltpu.CompilerParams(vmem_limit_bytes=12 * 1024 * 1024),
        cost_estimate=pl.CostEstimate(flops=3 * 10**9, bytes_accessed=10**7, transcendentals=0),
        name="skip",
    )(after, field, skip_weight, skip_bias)


def inverse(blocks, skipped, bias_rows):
    table = inverse_tables()
    return pl.pallas_call(
        inverse_kernel,
        out_specs=pl.BlockSpec(memory_space=pltpu.HBM),
        out_shape=jax.ShapeDtypeStruct((1, C, NX, ROWS_Y), BF16),
        scratch_shapes=[
            pltpu.VMEM((C, 2 * MODES, ROWS_Y), BF16),
            pltpu.VMEM((C, NX, ROWS_Y), BF16),
            pltpu.SemaphoreType.DMA((C // 2,)),
        ],
        compiler_params=pltpu.CompilerParams(vmem_limit_bytes=12 * 1024 * 1024),
        name="inverse",
    )(*blocks, skipped, jnp.asarray(table), bias_rows)


def solution(mesh):
    placed = (P("gz", None, None, "gy"), P(None, "gy", "gz", None), P(), P())
    return jax.shard_map(
        per_device, mesh=mesh, in_specs=placed, out_specs=P("gz", None, None, "gy"), check_vma=False
    )
```
